256 devices in a mesh: layer: 4 (over y), strip: 8 (over x, core), dir: 8 (over z).
Axes of the slice: x: 4, y: 4, z: 8, core: 2. Of those that a mesh axis runs over, the one named last changes fastest.
Arguments:
- screen: float32 [4, 2048, 4096], P('layer', 'strip', 'dir'), may hold values from -6 to 6
- innovation: bfloat16 [3, 4, 2048, 4096], P(None, 'layer', 'strip', 'dir'), may hold values from -6 to 6
- coef: float32 [4, 5, 4096], P('layer', None, 'dir'), may hold values from -2 to 2
- wind: int32 [4], P('layer'), may hold values from -2 to 2
- row_blocks: int32 [8, 4, 32], P(None, 'layer'), may hold values from 0 to 127, as said below
- table_index: int32 [8, 4], P(None, 'layer'), may hold values from 0 to 1
- row_table: bfloat16 [2, 512, 512], replicated, may hold values from -0.125 to 0.125
- column_table: bfloat16 [2, 512, 4096], P(None, None, 'dir'), may hold values from -0.09375 to 0.09375
Outputs:
- screen_out: float32 [4, 2048, 4096], P('layer', 'strip', 'dir')
- slopes: float32 [3, 2, 512, 8, 512], P(None, None, ('layer', 'strip'), 'dir')
The draws below stay inside these ranges and needn't reach their ends.
Inputs may be any that keep to these rules, and one draw needn't show every extreme that they name: `row_blocks`: for each direction and layer, 32 consecutive row blocks counted modulo 128.
All inputs are finite; a program needn't handle non-finite values.
Results may differ from the reference program's by a relative error of at most 0.0029.
Values sent between devices are 32-bit elements; how exact they have to be, the bound alone decides.
No kernel may reach another device: no remote copies, remote signals or barrier semaphores. Data moves between devices by JAX's collectives and lax.ppermute only.
A program may use at most 128 MiB of HBM per device.

```python
import jax
import jax.numpy as jnp
from jax import lax

PR = 512
PC = 512
BR = 16
NBR = 32
HB = 2
NM = 2
STEPS = 3
LAYERS = 4
NR = 2048
NC = 4096
NDIR = 8
NBLK = 128
FR = 512


def draw_row_blocks(key, part):
    key = jax.random.fold_in(key, 23)
    first, second = jax.random.split(key)
    starts = jax.random.randint(first, (NDIR * LAYERS,), 0, NBLK).astype(jnp.int32)
    marked = jax.random.randint(second, (), 0, NDIR * LAYERS).astype(jnp.int32)
    starts = jnp.where(jnp.arange(NDIR * LAYERS, dtype=jnp.int32) == marked, NBLK - 1, starts)
    blocks = (starts[:, None] + jnp.arange(NBR, dtype=jnp.int32)[None, :]) % NBLK
    return blocks.reshape(NDIR, LAYERS, NBR).astype(jnp.int32)


def place_ends(array, own_key, least, high):
    place = [jax.random.randint(jax.random.fold_in(own_key, axis), (), 0, length) for axis, length in enumerate(array.shape)]
    widest = array.shape.index(max(array.shape))
    neighbour = place[:widest] + [(place[widest] + 1) % array.shape[widest]] + place[widest + 1:]
    return array.at[tuple(place)].set(least).at[tuple(neighbour)].set(high)


def block_levels(key, dims, cuts, low, top_value):
    loudness, own = 1.0, jax.random.fold_in(key, 6)
    for axis_at, parts in cuts:
        draws = jnp.exp(jax.random.uniform(jax.random.fold_in(own, axis_at), (parts,), jnp.float32, low / len(cuts), top_value / len(cuts)))
        loudness = loudness * jnp.repeat(draws, dims[axis_at] // parts).reshape([-1 if axis == axis_at else 1 for axis in range(len(dims))])
    return loudness


def scatter_about(key, shape, scale, most, pieces=(), held_as=jnp.bfloat16):
    result = jax.random.normal(key, shape, jnp.float32) * scale
    if len(pieces) > 0:
        result = block_levels(key, shape, pieces, -0.22, 0.18) * result
    return jnp.clip(result, min=-most, max=most).astype(held_as)


def setup_inputs(seed: int = 0) -> dict:
    streams_of = jax.random.split(jax.random.key(seed), 9)
    return {
        "screen": scatter_about(streams_of[0], (LAYERS, NR, NC), 1.0, 6.0, ((0, 4), (1, 8), (2, 8)), jnp.float32),
        "innovation": scatter_about(streams_of[1], (STEPS, LAYERS, NR, NC), 1.0, 6.0, ((1, 4), (2, 8), (3, 8))),
        "coef": scatter_about(streams_of[2], (LAYERS, 2 * HB + 1, NC), 0.35, 2.0, ((0, 4), (2, 8)), jnp.float32),
        "wind": place_ends(jax.random.randint(streams_of[3], (LAYERS,), -HB, HB + 1), jax.random.fold_in(streams_of[3], 1), -HB, HB).astype(jnp.int32),
        "row_blocks": draw_row_blocks(jax.random.fold_in(streams_of[8], 71), 0),
        "table_index": place_ends(jax.random.randint(streams_of[5], (NDIR, LAYERS), 0, NM), jax.random.fold_in(streams_of[5], 1), 0, NM - 1).astype(jnp.int32),
        "row_table": scatter_about(streams_of[6], (NM, PR, FR), (FR * LAYERS) ** -0.5, 0.125),
        "column_table": scatter_about(streams_of[7], (NM, PC, NC), NC ** -0.5, 0.09375, ((2, 8),)),
    }


def reference(screen, innovation, coef, wind, row_blocks, table_index, row_table, column_table):
    highest = lax.Precision.HIGHEST
    foot_rows = (row_blocks[:, :, :, None] * BR + jnp.arange(BR, dtype=jnp.int32)).reshape(NDIR, LAYERS, FR).astype(jnp.int32)
    row_values = row_table.astype(jnp.float32)
    dir_iota = jnp.arange(NDIR, dtype=jnp.int32)[:, None]
    results = []
    for step_index in range(STEPS):
        layers_new = []
        for layer_index in range(LAYERS):
            total = innovation[step_index, layer_index].astype(jnp.float32)
            for tap_index in range(2 * HB + 1):
                moved = jnp.roll(screen[layer_index], wind[layer_index] - tap_index + HB, axis=0)
                total = total + coef[layer_index, tap_index][None, :] * moved
            layers_new.append(total)
        screen = jnp.stack(layers_new)
        flat = screen.astype(jnp.bfloat16)
        pupil = jnp.zeros((NDIR, PR, PC), jnp.float32)
        for layer_index in range(LAYERS):
            images = jnp.stack([jnp.dot(flat[layer_index], column_table[mat_index].T, preferred_element_type=jnp.float32) for mat_index in range(NM)])
            picks = table_index[:, layer_index]
            chosen = images[picks]
            foot = chosen[dir_iota, foot_rows[:, layer_index]]
            weights = row_values[picks]
            pupil = pupil + jnp.einsum('dpf,dfc->dpc', weights, foot, precision=highest)
        across = jnp.concatenate([pupil[:, :, 1:], jnp.zeros((NDIR, PR, 1), jnp.float32)], 2) - pupil
        below = jnp.concatenate([pupil[:, 1:], jnp.zeros((NDIR, 1, PC), jnp.float32)], 1) - pupil
        results.append(jnp.transpose(jnp.stack([across, below]), (0, 2, 1, 3)))
    return screen, jnp.stack(results)
```

```python
import jax
import jax.numpy as jnp
from jax import lax
from jax.experimental import pallas as pl
from jax.experimental.pallas import tpu as pltpu
from jax.sharding import PartitionSpec as P

ROWS = 256
COLS = 512
PR = 512
PC = 512
STEPS = 3
NM = 2
NDIR = 8
LAYERS = 4
STRIPS = 8
TAPS = 5
CHUNKS = LAYERS * STRIPS
PAD = 16
LANES = 128
GROUP = 6 * 8
PLANE = ("layer", "strip")
EVERY = ("layer", "strip", "dir")


def extrude_kernel(wind, screen, fresh, low, high, coef, table, images, screen_out, a, b, flat):
    step = pl.program_id(0)
    shift = wind[0] + 2

    def advance(src, start, count, fresh_rows):
        window = pltpu.roll(src[start - 8 : start + count + 8, :], shift, axis=0)
        total = fresh_rows.astype(jnp.float32)
        for k in range(TAPS):
            total = total + coef[k : k + 1, :] * window[8 + k : 8 + k + count, :]
        return total

    def inner(src, dst):
        for r in range(0, ROWS, 32):
            total = advance(src, PAD + r, 32, fresh[0, r : r + 32, :])
            flat[r : r + 32, :] = total.astype(jnp.bfloat16)
            dst(r, total)

    def keep_in(ref):
        def put(r, total):
            ref[PAD + r : PAD + r + 32, :] = total

        return put

    def put_out(r, total):
        screen_out[r : r + 32, :] = total

    @pl.when(step == 0)
    def _():
        a[0:PAD, :] = low[0:PAD, :]
        a[PAD : PAD + ROWS, :] = screen[...]
        a[PAD + ROWS :, :] = high[0:PAD, :]
        b[0:8, :] = jnp.zeros((8, COLS), jnp.float32)
        b[8:PAD, :] = advance(a, 8, 8, low[16:24, :])
        b[PAD + ROWS : PAD + ROWS + 8, :] = advance(a, PAD + ROWS, 8, high[16:24, :])
        b[PAD + ROWS + 8 :, :] = jnp.zeros((8, COLS), jnp.float32)
        inner(a, keep_in(b))

    @pl.when(step == 1)
    def _():
        a[8:PAD, :] = advance(b, 8, 8, low[24:32, :])
        a[PAD + ROWS : PAD + ROWS + 8, :] = advance(b, PAD + ROWS, 8, high[24:32, :])
        inner(b, keep_in(a))

    @pl.when(step == 2)
    def _():
        inner(a, put_out)

    rows = flat[...]
    for m in range(NM):
        image = lax.dot_general(
            table[m], rows, (((1,), (1,)), ((), ())), preferred_element_type=jnp.float32
        )
        for half in range(2):
            for part in range(2):
                piece = image[half * 256 : half * 256 + 256, part * LANES : part * LANES + LANES]
                images[:, part, 0, m, half, :, :] = piece.reshape(CHUNKS, 8, LANES)


def pupil_kernel(first, pick, x, row_table, out, feet, pupil):
    feet[...] = jnp.zeros(feet.shape, jnp.float32)
    lane = lax.broadcasted_iota(jnp.int32, (GROUP, LANES), 1)

    for d in range(NDIR):
        for layer in range(LAYERS):
            start = first[layer * NDIR + d]
            m = pick[layer * NDIR + d]
            block = start // 8
            shift = (start % 8) * 16
            back = (LANES - shift) % LANES
            rolled = []
            for i in range(5):
                rows = x[layer * 16 + (block + i) % 16, :, m]
                rolled.append(pltpu.roll(rows.reshape(GROUP, LANES), back, axis=1))
            for i in range(4):
                piece = jnp.where(lane < LANES - shift, rolled[i], rolled[i + 1])
                at = (m, pl.ds(d * GROUP, GROUP), pl.ds(i * LANES, LANES))
                feet[at] = feet[at] + piece

    for m in range(NM):
        whole = feet[m]
        head = whole.astype(jnp.bfloat16)
        tail = (whole - head.astype(jnp.float32)).astype(jnp.bfloat16)
        for at, part in enumerate((head, tail)):
            product = lax.dot_general(
                part, row_table[m], (((1,), (1,)), ((), ())), preferred_element_type=jnp.float32
            )
            if m == 0 and at == 0:
                pupil[...] = product
            else:
                pupil[...] = pupil[...] + product

    lane8 = lax.broadcasted_iota(jnp.int32, (8, LANES), 1)
    slot = lane8 // 16
    within = lane8 % 16

    for d in range(NDIR):
        heads = []
        for g in range(4):
            tiles = [
                pupil[d * GROUP + 8 * j : d * GROUP + 8 * j + 8, g * LANES : g * LANES + LANES]
                for j in range(6)
            ]
            gathered = tiles[0]
            for j in range(1, 6):
                gathered = jnp.where(within == j, pltpu.roll(tiles[j], j, axis=1), gathered)
            heads.append(gathered)
        for g in range(4):
            tiles = [
                pupil[d * GROUP + 8 * j : d * GROUP + 8 * j + 8, g * LANES : g * LANES + LANES]
                for j in range(6)
            ]
            for q in range(8):
                if q < 7:
                    edge = pltpu.roll(heads[g], (96 - 16 * (q + 1)) % LANES, axis=1)
                elif g < 3:
                    edge = pltpu.roll(heads[g + 1], 96, axis=1)
                else:
                    edge = jnp.zeros((8, LANES), jnp.float32)
                packed = edge
                for j in range(6):
                    turn = (16 * j - 16 * q) % LANES
                    moved = tiles[j] if turn == 0 else pltpu.roll(tiles[j], turn, axis=1)
                    packed = jnp.where(slot == j, moved, packed)
                out[(g * 8 + q) * NDIR + d] = packed


def slope_kernel(x, out):
    total = x[:, 0]
    for z in range(1, 8):
        total = total + x[:, z]
    flipped = jnp.transpose(total.reshape(CHUNKS * 8, LANES))
    for t in range(STEPS):
        left = flipped[32 * t : 32 * t + 16]
        right = flipped[32 * t + 16 : 32 * t + 32]
        rows = jnp.concatenate([left, right], axis=1)
        edge = jnp.concatenate(
            [flipped[96 + 2 * t : 97 + 2 * t], flipped[97 + 2 * t : 98 + 2 * t]], axis=1
        )
        beside = jnp.concatenate([rows[:, 1:], jnp.zeros((16, 1), jnp.float32)], axis=1)
        below = jnp.concatenate([rows[1:], edge], axis=0)
        out[t, 0] = beside - rows
        out[t, 1] = below - rows


def neighbours(count, by):
    return [(i, (i + by) % count) for i in range(count)]


def shards(screen, innovation, coef, wind, row_blocks, table_index, row_table, column_table):
    screen = screen[0]
    fresh = innovation[:, 0]
    strips = lax.axis_size("strip")

    last = jnp.concatenate(
        [
            screen[-16:],
            fresh[0, -8:].astype(jnp.float32),
            fresh[1, -8:].astype(jnp.float32),
        ],
        axis=0,
    )
    begin = jnp.concatenate(
        [
            screen[:16],
            fresh[0, :8].astype(jnp.float32),
            fresh[1, :8].astype(jnp.float32),
        ],
        axis=0,
    )
    low = lax.ppermute(last, "strip", neighbours(strips, 1))
    high = lax.ppermute(begin, "strip", neighbours(strips, -1))

    whole = lambda shape: pl.BlockSpec(shape, lambda t: (0,) * len(shape))
    images, screen_out = pl.pallas_call(
        extrude_kernel,
        grid=(STEPS,),
        in_specs=[
            pl.BlockSpec(memory_space=pltpu.SMEM),
            whole((ROWS, COLS)),
            pl.BlockSpec((1, ROWS, COLS), lambda t: (t, 0, 0)),
            whole((32, COLS)),
            whole((32, COLS)),
            whole((TAPS, COLS)),
            whole((NM, PC, COLS)),
        ],
        out_specs=[
            pl.BlockSpec(
                (CHUNKS, 2, 1, NM, 2, 8, LANES), lambda t: (0, 0, t, 0, 0, 0, 0)
            ),
            whole((ROWS, COLS)),
        ],
        out_shape=[
            jax.ShapeDtypeStruct((CHUNKS, 2, STEPS, NM, 2, 8, LANES), jnp.float32),
            jax.ShapeDtypeStruct((ROWS, COLS), jnp.float32),
        ],
        scratch_shapes=[
            pltpu.VMEM((ROWS + 2 * PAD, COLS), jnp.float32),
            pltpu.VMEM((ROWS + 2 * PAD, COLS), jnp.float32),
            pltpu.VMEM((ROWS, COLS), jnp.bfloat16),
        ],
        compiler_params=pltpu.CompilerParams(vmem_limit_bytes=40 * 1024 * 1024),
        name="extrude",
    )(wind, screen, fresh, low, high, coef[0], column_table)

    gathered = lax.all_to_all(images, PLANE, 0, 0, tiled=True)

    places = jnp.stack([row_blocks[:, 0, 0], table_index[:, 0]])
    places = lax.all_gather(places, "layer")
    first = places[:, 0].reshape(LAYERS * NDIR)
    pick = places[:, 1].reshape(LAYERS * NDIR)

    packed = pl.pallas_call(
        pupil_kernel,
        in_specs=[
            pl.BlockSpec(memory_space=pltpu.SMEM),
            pl.BlockSpec(memory_space=pltpu.SMEM),
            pl.BlockSpec(memory_space=pltpu.VMEM),
            pl.BlockSpec(memory_space=pltpu.VMEM),
        ],
        out_specs=pl.BlockSpec(memory_space=pltpu.VMEM),
        out_shape=jax.ShapeDtypeStruct((CHUNKS * NDIR, 8, LANES), jnp.float32),
        scratch_shapes=[
            pltpu.VMEM((NM, NDIR * GROUP, PR), jnp.float32),
            pltpu.VMEM((NDIR * GROUP, PR), jnp.float32),
        ],
        compiler_params=pltpu.CompilerParams(vmem_limit_bytes=40 * 1024 * 1024),
        name="pupil",
    )(first, pick, gathered.reshape(CHUNKS * 2, STEPS, NM, 2, 8, LANES), row_table)

    mine = lax.all_to_all(packed, EVERY, 0, 0, tiled=True)

    slopes = pl.pallas_call(
        slope_kernel,
        out_shape=jax.ShapeDtypeStruct((STEPS, 2, 16, PC), jnp.float32),
        in_specs=[pl.BlockSpec(memory_space=pltpu.VMEM)],
        out_specs=pl.BlockSpec(memory_space=pltpu.VMEM),
        compiler_params=pltpu.CompilerParams(vmem_limit_bytes=40 * 1024 * 1024),
        name="slopes",
    )(mine.reshape(CHUNKS, NDIR, 8, LANES))

    return (screen_out[None], slopes[:, :, :, None, :])


def solution(mesh):
    return jax.shard_map(
        shards,
        mesh=mesh,
        in_specs=(
            P("layer", "strip", "dir"),
            P(None, "layer", "strip", "dir"),
            P("layer", None, "dir"),
            P("layer"),
            P(None, "layer", None),
            P(None, "layer"),
            P(),
            P(None, None, "dir"),
        ),
        out_specs=(P("layer", "strip", "dir"), P(None, None, ("layer", "strip"), "dir", None)),
        check_vma=False,
    )
```

```python
import jax
import jax.numpy as jnp
from jax import lax
from jax.experimental import pallas as pl
from jax.experimental.pallas import tpu as pltpu
from jax.sharding import PartitionSpec as P

ROWS = 256
COLS = 512
PR = 512
PC = 512
STEPS = 3
NM = 2
NDIR = 8
LAYERS = 4
STRIPS = 8
TAPS = 5
CHUNKS = LAYERS * STRIPS
PAD = 16
LANES = 128
GROUP = STEPS * 2 * 8
PLANE = ("layer", "strip")


def advance(window, fresh, coef, shift):
    count = fresh.shape[0]
    moved = pltpu.roll(window, shift, axis=0)
    total = fresh.astype(jnp.float32)
    for k in range(TAPS):
        total = total + coef[k] * moved[8 + k : 8 + k + count, :]
    return total


def inner_kernel(
    wind, screen, fresh, coef, column_table, flats, near0, fresh0, near1, near2, near3, table, taps, s3, s1, s2
):
    shift = wind[0] + 2
    table[...] = column_table[...]
    taps[...] = coef[...]
    near0[0] = screen[0:16, :]
    near0[1] = screen[ROWS - 16 : ROWS, :]
    fresh0[0] = fresh[:, 0:32, :]
    fresh0[1] = fresh[:, ROWS - 32 : ROWS, :]
    steps = ((screen, s1, near1, 16, 16), (s1, s2, near2, 16, 16), (s2, s3, near3, 8, 32))
    for t, (src, dst, near, count, flat) in enumerate(steps):
        begin, end = 8 * (t + 1), ROWS - 8 * (t + 1)
        for r in range(begin, end, 32):
            stop = min(r + 32, end)
            dst[r:stop, :] = advance(src[r - 8 : stop + 8, :], fresh[t, r:stop, :], coef, shift)
        near[0:count, :] = dst[begin : begin + count, :]
        near[count:, :] = dst[end - count : end, :]
        for r in range(flat, ROWS - flat, 32):
            stop = min(r + 32, ROWS - flat)
            flats[t, r:stop, :] = dst[r:stop, :].astype(jnp.bfloat16)


def outer_kernel(
    wind,
    near0,
    fresh0,
    low,
    high,
    coef,
    near1,
    near2,
    near3,
    table,
    inside,
    old,
    images,
    screen_out,
    flat,
    piece,
    ends,
    sem,
):
    shift = wind[0] + 2
    none = jnp.zeros((8, COLS), jnp.float32)
    join = lambda *rows: jnp.concatenate(rows, axis=0)
    after = lambda window, fresh: advance(window, fresh, coef, shift)
    def project(t):
        for m in range(NM):
            image = lax.dot_general(
                table[m], flat[t], (((1,), (1,)), ((), ())), preferred_element_type=jnp.float32
            )
            for half in range(2):
                for part in range(2):
                    at = image[half * 256 : half * 256 + 256, part * LANES : part * LANES + LANES]
                    piece[t, :, part, m, half, :, :] = at.reshape(CHUNKS, 8, LANES)
        copy = pltpu.make_async_copy(piece.at[t], images.at[:, :, t], sem.at[t])
        copy.start()
        return copy

    first, final = fresh0[0, 0].astype(jnp.float32), fresh0[1, 0].astype(jnp.float32)
    e = after(join(low[0:16, :], near0[0]), join(low[16:24, :], first[0:8]))
    f = after(join(near0[1], high[0:16, :]), join(final[24:32], high[16:24, :]))
    flat[0] = inside[0]
    flat[0, 0:16, :] = join(e[8:16], near1[0:8, :]).astype(jnp.bfloat16)
    flat[0, ROWS - 16 : ROWS, :] = join(near1[24:32, :], f[0:8]).astype(jnp.bfloat16)
    leave = [project(0)]

    first, final = fresh0[0, 1].astype(jnp.float32), fresh0[1, 1].astype(jnp.float32)
    e = after(join(none, e, near1[0:16, :]), join(low[24:32, :], first[0:16]))
    f = after(join(near1[16:32, :], f, none), join(final[16:32], high[24:32, :]))
    flat[1] = inside[1]
    flat[1, 0:16, :] = e[8:24].astype(jnp.bfloat16)
    flat[1, ROWS - 16 : ROWS, :] = f[0:16].astype(jnp.bfloat16)
    leave.append(project(1))

    first, final = fresh0[0, 2].astype(jnp.float32), fresh0[1, 2].astype(jnp.float32)
    e = after(join(e, near2[0:16, :]), first[0:24])
    f = after(join(near2[16:32, :], f), final[8:32])
    ends[0] = e
    ends[1] = f
    leave += [
        pltpu.make_async_copy(ends.at[0], screen_out.at[pl.ds(0, 24), :], sem.at[3]),
        pltpu.make_async_copy(ends.at[1], screen_out.at[pl.ds(ROWS - 24, 24), :], sem.at[4]),
    ]
    leave[-2].start()
    leave[-1].start()
    flat[2] = inside[2]
    flat[2, 0:32, :] = join(e, near3[0:8, :]).astype(jnp.bfloat16)
    flat[2, ROWS - 32 : ROWS, :] = join(near3[8:16, :], f).astype(jnp.bfloat16)
    leave.append(project(2))
    for copy in leave:
        copy.wait()


def pupil_kernel(mine, places, x, table, *refs):
    *outs, feet, pupils = refs
    feet[...] = jnp.zeros(feet.shape, jnp.float32)
    lane = lax.broadcasted_iota(jnp.int32, (GROUP, LANES), 1)

    for layer in range(LAYERS):
        for d in range(NDIR):
            start = places[layer * 2 * NDIR + d]
            m = places[(layer * 2 + 1) * NDIR + d]
            block = start // 8
            shift = (start % 8) * 16
            back = (LANES - shift) % LANES
            rolled = []
            for i in range(5):
                rows = x[layer * 16 + (block + i) % 16, :, m]
                rolled.append(pltpu.roll(rows.reshape(GROUP, LANES), back, axis=1))
            for i in range(4):
                piece = jnp.where(lane < LANES - shift, rolled[i], rolled[i + 1])
                at = (m, pl.ds(d * GROUP, GROUP), pl.ds(i * LANES, LANES))
                feet[at] = feet[at] + piece

    total = None
    for m in range(NM):
        whole = feet[m]
        head = whole.astype(jnp.bfloat16)
        tail = (whole - head.astype(jnp.float32)).astype(jnp.bfloat16)
        for part in (head, tail):
            product = lax.dot_general(
                part, table[m], (((1,), (1,)), ((), ())), preferred_element_type=jnp.float32
            )
            total = product if total is None else total + product
    pupils[...] = total.reshape(pupils.shape)
    for j, out in enumerate(outs):
        out[...] = pupils[(mine[0] + j) % NDIR]


def pack_kernel(x, y, z, out):
    total = x[...] + y[...] + z[...]
    tiles = [total[8 * j : 8 * j + 8] for j in range(6)]

    lane = lax.broadcasted_iota(jnp.int32, (8, LANES), 1)
    slot = lane // 16
    within = lane % 16
    heads = []
    for g in range(4):
        gathered = tiles[0][:, g * LANES : g * LANES + LANES]
        for j in range(1, 6):
            moved = pltpu.roll(tiles[j][:, g * LANES : g * LANES + LANES], j, axis=1)
            gathered = jnp.where(within == j, moved, gathered)
        heads.append(gathered)
    for g in range(4):
        for q in range(8):
            if q < 7:
                packed = pltpu.roll(heads[g], (96 - 16 * (q + 1)) % LANES, axis=1)
            elif g < 3:
                packed = pltpu.roll(heads[g + 1], 96, axis=1)
            else:
                packed = jnp.zeros((8, LANES), jnp.float32)
            for j in range(6):
                turn = (16 * j - 16 * q) % LANES
                moved = tiles[j][:, g * LANES : g * LANES + LANES]
                moved = moved if turn == 0 else pltpu.roll(moved, turn, axis=1)
                packed = jnp.where(slot == j, moved, packed)
            out[g * 8 + q] = packed


def slope_kernel(x, out):
    flipped = jnp.transpose(x[...].reshape(CHUNKS * 8, LANES))
    for t in range(STEPS):
        left = flipped[32 * t : 32 * t + 16]
        right = flipped[32 * t + 16 : 32 * t + 32]
        rows = jnp.concatenate([left, right], axis=1)
        edge = jnp.concatenate(
            [flipped[96 + 2 * t : 97 + 2 * t], flipped[97 + 2 * t : 98 + 2 * t]], axis=1
        )
        beside = jnp.concatenate([rows[:, 1:], jnp.zeros((16, 1), jnp.float32)], axis=1)
        below = jnp.concatenate([rows[1:], edge], axis=0)
        out[t, 0] = (beside - rows).reshape(16, 1, PC)
        out[t, 1] = (below - rows).reshape(16, 1, PC)


def neighbours(count, by):
    return [(i, (i + by) % count) for i in range(count)]


SCALARS = pl.BlockSpec(memory_space=pltpu.SMEM)


def room(mib):
    return pltpu.CompilerParams(vmem_limit_bytes=int(mib * 1024 * 1024))


def whole(*shape):
    return pl.BlockSpec(shape, lambda *_: (0,) * len(shape))


def shards(screen, innovation, coef, wind, row_blocks, table_index, row_table, column_table):
    state = screen[0]
    fresh = innovation[:, 0]
    taps = jnp.swapaxes(coef, 0, 1)
    strips = lax.axis_size("strip")

    last = [state[-16:], fresh[0, -8:].astype(jnp.float32), fresh[1, -8:].astype(jnp.float32)]
    begin = [state[:16], fresh[0, :8].astype(jnp.float32), fresh[1, :8].astype(jnp.float32)]
    low = lax.ppermute(jnp.concatenate(last, axis=0), "strip", neighbours(strips, 1))
    high = lax.ppermute(jnp.concatenate(begin, axis=0), "strip", neighbours(strips, -1))

    near = jax.ShapeDtypeStruct((32, COLS), jnp.float32)
    *inside, unfinished = pl.pallas_call(
        inner_kernel,
        in_specs=[
            SCALARS,
            whole(ROWS, COLS),
            whole(STEPS, ROWS, COLS),
            whole(TAPS, 1, COLS),
            whole(NM, PC, COLS),
        ],
        out_specs=[
            whole(STEPS, ROWS, COLS),
            whole(2, 16, COLS),
            whole(2, STEPS, 32, COLS),
            whole(32, COLS),
            whole(32, COLS),
            whole(16, COLS),
            whole(NM, PC, COLS),
            whole(TAPS, 1, COLS),
            whole(ROWS, COLS),
        ],
        out_shape=[
            jax.ShapeDtypeStruct((STEPS, ROWS, COLS), jnp.bfloat16),
            jax.ShapeDtypeStruct((2, 16, COLS), jnp.float32),
            jax.ShapeDtypeStruct((2, STEPS, 32, COLS), jnp.bfloat16),
            near,
            near,
            jax.ShapeDtypeStruct((16, COLS), jnp.float32),
            jax.ShapeDtypeStruct((NM, PC, COLS), jnp.bfloat16),
            jax.ShapeDtypeStruct((TAPS, 1, COLS), jnp.float32),
            jax.ShapeDtypeStruct((ROWS, COLS), jnp.float32),
        ],
        scratch_shapes=[pltpu.VMEM((ROWS, COLS), jnp.float32)] * 2,
        compiler_params=room(50),
        cost_estimate=pl.CostEstimate(
            flops=12 * STEPS * ROWS * COLS, bytes_accessed=14 * ROWS * COLS, transcendentals=0
        ),
        name="inner",
    )(wind, state, fresh, taps, column_table)

    anywhere = pl.BlockSpec(memory_space=pl.ANY)
    images, screen_out = pl.pallas_call(
        outer_kernel,
        in_specs=[
            SCALARS,
            whole(2, 16, COLS),
            whole(2, STEPS, 32, COLS),
            whole(32, COLS),
            whole(32, COLS),
            whole(TAPS, 1, COLS),
            whole(32, COLS),
            whole(32, COLS),
            whole(16, COLS),
            whole(NM, PC, COLS),
            whole(STEPS, ROWS, COLS),
            anywhere,
        ],
        out_specs=[anywhere, anywhere],
        out_shape=[
            jax.ShapeDtypeStruct((CHUNKS, 2, STEPS, NM, 2, 8, LANES), jnp.float32),
            jax.ShapeDtypeStruct((ROWS, COLS), jnp.float32),
        ],
        input_output_aliases={11: 1},
        scratch_shapes=[
            pltpu.VMEM((STEPS, ROWS, COLS), jnp.bfloat16),
            pltpu.VMEM((STEPS, CHUNKS, 2, NM, 2, 8, LANES), jnp.float32),
            pltpu.VMEM((2, 24, COLS), jnp.float32),
            pltpu.SemaphoreType.DMA((5,)),
        ],
        compiler_params=room(50),
        name="outer",
    )(
        wind,
        *inside[1:3],
        low,
        high,
        inside[7],
        *inside[3:7],
        inside[0],
        unfinished,
    )

    gathered = lax.all_to_all(images, PLANE, 0, 0, tiled=True)
    places = jnp.stack([row_blocks[:, 0, 0], table_index[:, 0]])
    places = lax.all_gather(places, "layer").reshape(LAYERS * 2 * NDIR)
    mine = lax.axis_index("dir").astype(jnp.int32).reshape(1)
    pupils = pl.pallas_call(
        pupil_kernel,
        in_specs=[
            SCALARS,
            SCALARS,
            whole(CHUNKS * 2, STEPS, NM, 2, 8, LANES),
            whole(NM, PR, PR),
        ],
        out_specs=[whole(GROUP, PR)] * NDIR,
        out_shape=[jax.ShapeDtypeStruct((GROUP, PR), jnp.float32)] * NDIR,
        scratch_shapes=[
            pltpu.VMEM((NM, NDIR * GROUP, PR), jnp.float32),
            pltpu.VMEM((NDIR, GROUP, PR), jnp.float32),
        ],
        compiler_params=room(24),
        name="pupil",
    )(mine, places, gathered.reshape(CHUNKS * 2, STEPS, NM, 2, 8, LANES), row_table)

    count = lax.axis_size("dir")
    up = lambda x: lax.ppermute(x, "dir", neighbours(count, 1))
    down = lambda x: lax.ppermute(x, "dir", neighbours(count, -1))
    rising = up(pupils[4])
    falling = down(pupils[5])
    rising = up(pupils[3] + rising)
    falling = down(pupils[6] + falling)
    rising = up(pupils[2] + rising)
    falling = down(pupils[7] + falling)
    rising = up(pupils[1] + rising)
    packed = pl.pallas_call(
        pack_kernel,
        in_specs=[whole(GROUP, PR)] * 3,
        out_specs=whole(CHUNKS, 8, LANES),
        out_shape=jax.ShapeDtypeStruct((CHUNKS, 8, LANES), jnp.float32),
        compiler_params=room(16),
        name="pack",
    )(pupils[0], rising, falling)
    rows = lax.all_to_all(packed, PLANE, 0, 0, tiled=True)
    slopes = pl.pallas_call(
        slope_kernel,
        in_specs=[whole(CHUNKS, 8, LANES)],
        out_specs=whole(STEPS, 2, 16, 1, PC),
        out_shape=jax.ShapeDtypeStruct((STEPS, 2, 16, 1, PC), jnp.float32),
        compiler_params=room(16),
        name="slopes",
    )(rows)
    return (screen_out[None], slopes)


def solution(mesh):
    return jax.shard_map(
        shards,
        mesh=mesh,
        in_specs=(
            P("layer", "strip", "dir"),
            P(None, "layer", "strip", "dir"),
            P("layer", None, "dir"),
            P("layer"),
            P(None, "layer", None),
            P(None, "layer"),
            P(),
            P(None, None, "dir"),
        ),
        out_specs=(P("layer", "strip", "dir"), P(None, None, ("layer", "strip"), "dir", None)),
        check_vma=False,
    )
```

```python
import jax
import jax.numpy as jnp
from jax import lax
from jax.experimental import pallas as pl
from jax.experimental.pallas import tpu as pltpu
from jax.sharding import PartitionSpec as P

ROWS = 256
COLS = 512
PR = 512
PC = 512
STEPS = 3
NM = 2
NDIR = 8
LAYERS = 4
STRIPS = 8
TAPS = 5
CHUNKS = LAYERS * STRIPS
PAD = 16
LANES = 128
GROUP = STEPS * 2 * 8
PLANE = ("layer", "strip")


def advance(window, fresh, coef, shift):
    count = fresh.shape[0]
    moved = pltpu.roll(window, shift, axis=0)
    total = fresh.astype(jnp.float32)
    for k in range(TAPS):
        total = total + coef[k] * moved[8 + k : 8 + k + count, :]
    return total


def ends_kernel(screen, fresh, coef, begin, last, screen_on, fresh_on, coef_on):
    begin[0:16, :] = screen[0:16, :]
    last[0:16, :] = screen[ROWS - 16 : ROWS, :]
    for t in range(2):
        at = slice(16 + 8 * t, 24 + 8 * t)
        begin[at, :] = fresh[t, 0:16, :].astype(jnp.float32)[0:8, :]
        last[at, :] = fresh[t, ROWS - 16 : ROWS, :].astype(jnp.float32)[8:16, :]
    screen_on[...] = screen[...]
    fresh_on[...] = fresh[...]
    coef_on[...] = coef[...]


def inner_kernel(
    wind, screen, fresh, coef, flats, near0, fresh0, near1, near2, near3, s3, s1, s2
):
    shift = wind[0] + 2
    near0[0] = screen[0:16, :]
    near0[1] = screen[ROWS - 16 : ROWS, :]
    fresh0[0] = fresh[:, 0:32, :]
    fresh0[1] = fresh[:, ROWS - 32 : ROWS, :]
    steps = ((screen, s1, near1, 16, 16), (s1, s2, near2, 16, 16), (s2, s3, near3, 8, 32))
    for t, (src, dst, near, count, flat) in enumerate(steps):
        begin, end = 8 * (t + 1), ROWS - 8 * (t + 1)
        for r in range(begin, end, 32):
            stop = min(r + 32, end)
            dst[r:stop, :] = advance(src[r - 8 : stop + 8, :], fresh[t, r:stop, :], coef, shift)
        near[0:count, :] = dst[begin : begin + count, :]
        near[count:, :] = dst[end - count : end, :]
        for r in range(flat, ROWS - flat, 32):
            stop = min(r + 32, ROWS - flat)
            flats[t, r:stop, :] = dst[r:stop, :].astype(jnp.bfloat16)


def outer_kernel(
    wind,
    near0,
    fresh0,
    low,
    high,
    coef,
    near1,
    near2,
    near3,
    table,
    inside,
    old,
    images,
    screen_out,
    flat,
    piece,
    ends,
    sem,
):
    shift = wind[0] + 2
    none = jnp.zeros((8, COLS), jnp.float32)
    join = lambda *rows: jnp.concatenate(rows, axis=0)
    after = lambda window, fresh: advance(window, fresh, coef, shift)
    def project(t):
        for m in range(NM):
            image = lax.dot_general(
                table[m], flat[t], (((1,), (1,)), ((), ())), preferred_element_type=jnp.float32
            )
            for half in range(2):
                for part in range(2):
                    at = image[half * 256 : half * 256 + 256, part * LANES : part * LANES + LANES]
                    piece[t, :, part, m, half, :, :] = at.reshape(CHUNKS, 8, LANES)
        copy = pltpu.make_async_copy(piece.at[t], images.at[:, :, t], sem.at[t])
        copy.start()
        return copy

    first, final = fresh0[0, 0].astype(jnp.float32), fresh0[1, 0].astype(jnp.float32)
    e = after(join(low[0:16, :], near0[0]), join(low[16:24, :], first[0:8]))
    f = after(join(near0[1], high[0:16, :]), join(final[24:32], high[16:24, :]))
    flat[0] = inside[0]
    flat[0, 0:16, :] = join(e[8:16], near1[0:8, :]).astype(jnp.bfloat16)
    flat[0, ROWS - 16 : ROWS, :] = join(near1[24:32, :], f[0:8]).astype(jnp.bfloat16)
    leave = [project(0)]

    first, final = fresh0[0, 1].astype(jnp.float32), fresh0[1, 1].astype(jnp.float32)
    e = after(join(none, e, near1[0:16, :]), join(low[24:32, :], first[0:16]))
    f = after(join(near1[16:32, :], f, none), join(final[16:32], high[24:32, :]))
    flat[1] = inside[1]
    flat[1, 0:16, :] = e[8:24].astype(jnp.bfloat16)
    flat[1, ROWS - 16 : ROWS, :] = f[0:16].astype(jnp.bfloat16)
    leave.append(project(1))

    first, final = fresh0[0, 2].astype(jnp.float32), fresh0[1, 2].astype(jnp.float32)
    e = after(join(e, near2[0:16, :]), first[0:24])
    f = after(join(near2[16:32, :], f), final[8:32])
    ends[0] = e
    ends[1] = f
    leave += [
        pltpu.make_async_copy(ends.at[0], screen_out.at[pl.ds(0, 24), :], sem.at[3]),
        pltpu.make_async_copy(ends.at[1], screen_out.at[pl.ds(ROWS - 24, 24), :], sem.at[4]),
    ]
    leave[-2].start()
    leave[-1].start()
    flat[2] = inside[2]
    flat[2, 0:32, :] = join(e, near3[0:8, :]).astype(jnp.bfloat16)
    flat[2, ROWS - 32 : ROWS, :] = join(near3[8:16, :], f).astype(jnp.bfloat16)
    leave.append(project(2))
    for copy in leave:
        copy.wait()


def feet_kernel(places, x, feet):
    feet[...] = jnp.zeros(feet.shape, jnp.float32)
    lane = lax.broadcasted_iota(jnp.int32, (GROUP, LANES), 1)

    for layer in range(LAYERS):
        for d in range(NDIR):
            start = places[layer * 2 * NDIR + d]
            m = places[(layer * 2 + 1) * NDIR + d]
            block = start // 8
            shift = (start % 8) * 16
            back = (LANES - shift) % LANES
            rolled = []
            for i in range(5):
                rows = x[layer * 16 + (block + i) % 16, :, m]
                rolled.append(pltpu.roll(rows.reshape(GROUP, LANES), back, axis=1))
            for i in range(4):
                piece = jnp.where(lane < LANES - shift, rolled[i], rolled[i + 1])
                at = (m, pl.ds(d * GROUP, GROUP), pl.ds(i * LANES, LANES))
                feet[at] = feet[at] + piece


def pupil_kernel(mine, feet, table, *refs):
    *outs, pupils = refs
    total = None
    for m in range(NM):
        whole = feet[m]
        head = whole.astype(jnp.bfloat16)
        tail = (whole - head.astype(jnp.float32)).astype(jnp.bfloat16)
        for part in (head, tail):
            product = lax.dot_general(
                part, table[m], (((1,), (1,)), ((), ())), preferred_element_type=jnp.float32
            )
            total = product if total is None else total + product
    pupils[...] = total.reshape(pupils.shape)
    for j, out in enumerate(outs):
        out[...] = pupils[(mine[0] + j) % NDIR]


def pack_kernel(*refs):
    *terms, out = refs
    total = terms[0][...]
    for term in terms[1:]:
        total = total + term[...]
    tiles = [total[8 * j : 8 * j + 8] for j in range(6)]

    lane = lax.broadcasted_iota(jnp.int32, (8, LANES), 1)
    slot = lane // 16
    within = lane % 16
    heads = []
    for g in range(4):
        gathered = tiles[0][:, g * LANES : g * LANES + LANES]
        for j in range(1, 6):
            moved = pltpu.roll(tiles[j][:, g * LANES : g * LANES + LANES], j, axis=1)
            gathered = jnp.where(within == j, moved, gathered)
        heads.append(gathered)
    for g in range(4):
        for q in range(8):
            if q < 7:
                packed = pltpu.roll(heads[g], (96 - 16 * (q + 1)) % LANES, axis=1)
            elif g < 3:
                packed = pltpu.roll(heads[g + 1], 96, axis=1)
            else:
                packed = jnp.zeros((8, LANES), jnp.float32)
            for j in range(6):
                turn = (16 * j - 16 * q) % LANES
                moved = tiles[j][:, g * LANES : g * LANES + LANES]
                moved = moved if turn == 0 else pltpu.roll(moved, turn, axis=1)
                packed = jnp.where(slot == j, moved, packed)
            out[g * 8 + q] = packed


def slope_kernel(x, out):
    flipped = jnp.transpose(x[...].reshape(CHUNKS * 8, LANES))
    for t in range(STEPS):
        left = flipped[32 * t : 32 * t + 16]
        right = flipped[32 * t + 16 : 32 * t + 32]
        rows = jnp.concatenate([left, right], axis=1)
        edge = jnp.concatenate(
            [flipped[96 + 2 * t : 97 + 2 * t], flipped[97 + 2 * t : 98 + 2 * t]], axis=1
        )
        beside = jnp.concatenate([rows[:, 1:], jnp.zeros((16, 1), jnp.float32)], axis=1)
        below = jnp.concatenate([rows[1:], edge], axis=0)
        out[t, 0] = (beside - rows).reshape(16, 1, PC)
        out[t, 1] = (below - rows).reshape(16, 1, PC)


def neighbours(count, by):
    return [(i, (i + by) % count) for i in range(count)]


SCALARS = pl.BlockSpec(memory_space=pltpu.SMEM)


def room(mib):
    return pltpu.CompilerParams(vmem_limit_bytes=int(mib * 1024 * 1024))


def whole(*shape):
    return pl.BlockSpec(shape, lambda *_: (0,) * len(shape))


def shards(screen, innovation, coef, wind, row_blocks, table_index, row_table, column_table):
    state = screen[0]
    fresh = innovation[:, 0]
    strips = lax.axis_size("strip")

    near = jax.ShapeDtypeStruct((32, COLS), jnp.float32)
    taps = jax.ShapeDtypeStruct((TAPS, 1, COLS), jnp.float32)
    begin, last, state, fresh, taps = pl.pallas_call(
        ends_kernel,
        in_specs=[whole(ROWS, COLS), whole(STEPS, ROWS, COLS), whole(TAPS, 1, COLS)],
        out_specs=[
            whole(32, COLS),
            whole(32, COLS),
            whole(ROWS, COLS),
            whole(STEPS, ROWS, COLS),
            whole(TAPS, 1, COLS),
        ],
        out_shape=[
            near,
            near,
            jax.ShapeDtypeStruct((ROWS, COLS), jnp.float32),
            jax.ShapeDtypeStruct((STEPS, ROWS, COLS), jnp.bfloat16),
            taps,
        ],
        compiler_params=room(24),
        name="ends",
    )(state, fresh, jnp.swapaxes(coef, 0, 1))
    low = lax.ppermute(last, "strip", neighbours(strips, 1))
    high = lax.ppermute(begin, "strip", neighbours(strips, -1))

    *inside, unfinished = pl.pallas_call(
        inner_kernel,
        in_specs=[
            SCALARS,
            whole(ROWS, COLS),
            whole(STEPS, ROWS, COLS),
            whole(TAPS, 1, COLS),
        ],
        out_specs=[
            whole(STEPS, ROWS, COLS),
            whole(2, 16, COLS),
            whole(2, STEPS, 32, COLS),
            whole(32, COLS),
            whole(32, COLS),
            whole(16, COLS),
            whole(ROWS, COLS),
        ],
        out_shape=[
            jax.ShapeDtypeStruct((STEPS, ROWS, COLS), jnp.bfloat16),
            jax.ShapeDtypeStruct((2, 16, COLS), jnp.float32),
            jax.ShapeDtypeStruct((2, STEPS, 32, COLS), jnp.bfloat16),
            near,
            near,
            jax.ShapeDtypeStruct((16, COLS), jnp.float32),
            jax.ShapeDtypeStruct((ROWS, COLS), jnp.float32),
        ],
        scratch_shapes=[pltpu.VMEM((ROWS, COLS), jnp.float32)] * 2,
        compiler_params=room(24),
        cost_estimate=pl.CostEstimate(
            flops=12 * STEPS * ROWS * COLS, bytes_accessed=100 * ROWS * COLS, transcendentals=0
        ),
        name="inner",
    )(wind, state, fresh, taps)

    anywhere = pl.BlockSpec(memory_space=pl.ANY)
    images, screen_out = pl.pallas_call(
        outer_kernel,
        in_specs=[
            SCALARS,
            whole(2, 16, COLS),
            whole(2, STEPS, 32, COLS),
            whole(32, COLS),
            whole(32, COLS),
            whole(TAPS, 1, COLS),
            whole(32, COLS),
            whole(32, COLS),
            whole(16, COLS),
            whole(NM, PC, COLS),
            whole(STEPS, ROWS, COLS),
            anywhere,
        ],
        out_specs=[anywhere, anywhere],
        out_shape=[
            jax.ShapeDtypeStruct((CHUNKS, 2, STEPS, NM, 2, 8, LANES), jnp.float32),
            jax.ShapeDtypeStruct((ROWS, COLS), jnp.float32),
        ],
        input_output_aliases={11: 1},
        scratch_shapes=[
            pltpu.VMEM((STEPS, ROWS, COLS), jnp.bfloat16),
            pltpu.VMEM((STEPS, CHUNKS, 2, NM, 2, 8, LANES), jnp.float32),
            pltpu.VMEM((2, 24, COLS), jnp.float32),
            pltpu.SemaphoreType.DMA((5,)),
        ],
        compiler_params=room(50),
        name="outer",
    )(
        wind,
        *inside[1:3],
        low,
        high,
        taps,
        *inside[3:6],
        column_table,
        inside[0],
        unfinished,
    )

    gathered = lax.all_to_all(images, PLANE, 0, 0, tiled=True)
    places = jnp.stack([row_blocks[:, 0, 0], table_index[:, 0]])
    places = lax.all_gather(places, "layer").reshape(LAYERS * 2 * NDIR)
    mine = lax.axis_index("dir").astype(jnp.int32).reshape(1)
    feet = pl.pallas_call(
        feet_kernel,
        in_specs=[SCALARS, whole(CHUNKS * 2, STEPS, NM, 2, 8, LANES)],
        out_specs=whole(NM, NDIR * GROUP, PR),
        out_shape=jax.ShapeDtypeStruct((NM, NDIR * GROUP, PR), jnp.float32),
        compiler_params=room(24),
        cost_estimate=pl.CostEstimate(flops=0, bytes_accessed=100 * ROWS * COLS, transcendentals=0),
        name="feet",
    )(places, gathered.reshape(CHUNKS * 2, STEPS, NM, 2, 8, LANES))
    pupils = pl.pallas_call(
        pupil_kernel,
        in_specs=[SCALARS, whole(NM, NDIR * GROUP, PR), whole(NM, PR, PR)],
        out_specs=[whole(GROUP, PR)] * NDIR,
        out_shape=[jax.ShapeDtypeStruct((GROUP, PR), jnp.float32)] * NDIR,
        scratch_shapes=[pltpu.VMEM((NDIR, GROUP, PR), jnp.float32)],
        compiler_params=room(24),
        name="pupil",
    )(mine, feet, row_table)

    count = lax.axis_size("dir")
    terms = [pupils[0]] + [
        lax.ppermute(pupils[j], "dir", neighbours(count, j)) for j in (4, 3, 5, 2, 6, 1, 7)
    ]
    packed = pl.pallas_call(
        pack_kernel,
        in_specs=[whole(GROUP, PR)] * NDIR,
        out_specs=whole(CHUNKS, 8, LANES),
        out_shape=jax.ShapeDtypeStruct((CHUNKS, 8, LANES), jnp.float32),
        compiler_params=room(16),
        name="pack",
    )(*terms)
    rows = lax.all_to_all(packed, PLANE, 0, 0, tiled=True)
    slopes = pl.pallas_call(
        slope_kernel,
        in_specs=[whole(CHUNKS, 8, LANES)],
        out_specs=whole(STEPS, 2, 16, 1, PC),
        out_shape=jax.ShapeDtypeStruct((STEPS, 2, 16, 1, PC), jnp.float32),
        compiler_params=room(16),
        name="slopes",
    )(rows)
    return (screen_out[None], slopes)


def solution(mesh):
    return jax.shard_map(
        shards,
        mesh=mesh,
        in_specs=(
            P("layer", "strip", "dir"),
            P(None, "layer", "strip", "dir"),
            P("layer", None, "dir"),
            P("layer"),
            P(None, "layer", None),
            P(None, "layer"),
            P(),
            P(None, None, "dir"),
        ),
        out_specs=(P("layer", "strip", "dir"), P(None, None, ("layer", "strip"), "dir", None)),
        check_vma=False,
    )
```

```python
import jax
import jax.numpy as jnp
from jax import lax
from jax.experimental import pallas as pl
from jax.experimental.pallas import tpu as pltpu
from jax.sharding import PartitionSpec as P

ROWS = 256
COLS = 512
PR = 512
PC = 512
STEPS = 3
NM = 2
NDIR = 8
LAYERS = 4
STRIPS = 8
TAPS = 5
CHUNKS = LAYERS * STRIPS
PAD = 16
LANES = 128
GROUP = STEPS * 2 * 8
PLANE = ("layer", "strip")
PARTS = ((0,), (1,), (2,), (3,), (4,), (5,), (6,), (7,))


def advance(window, fresh, coef, shift):
    count = fresh.shape[0]
    moved = pltpu.roll(window, shift, axis=0)
    total = fresh.astype(jnp.float32)
    for k in range(TAPS):
        total = total + coef[k] * moved[8 + k : 8 + k + count, :]
    return total


def ends_kernel(screen, fresh, coef, begin, last, screen_on, fresh_on, coef_on):
    begin[0:16, :] = screen[0:16, :]
    last[0:16, :] = screen[ROWS - 16 : ROWS, :]
    for t in range(2):
        at = slice(16 + 8 * t, 24 + 8 * t)
        begin[at, :] = fresh[t, 0:16, :].astype(jnp.float32)[0:8, :]
        last[at, :] = fresh[t, ROWS - 16 : ROWS, :].astype(jnp.float32)[8:16, :]
    screen_on[...] = screen[...]
    fresh_on[...] = fresh[...]
    coef_on[...] = coef[...]


def inner_kernel(
    wind, screen, fresh, coef, flats, near0, fresh0, near1, near2, near3, s3, s1, s2
):
    shift = wind[0] + 2
    near0[0] = screen[0:16, :]
    near0[1] = screen[ROWS - 16 : ROWS, :]
    fresh0[0] = fresh[:, 0:32, :]
    fresh0[1] = fresh[:, ROWS - 32 : ROWS, :]
    steps = ((screen, s1, near1, 16, 16), (s1, s2, near2, 16, 16), (s2, s3, near3, 8, 32))
    for t, (src, dst, near, count, flat) in enumerate(steps):
        begin, end = 8 * (t + 1), ROWS - 8 * (t + 1)
        for r in range(begin, end, 32):
            stop = min(r + 32, end)
            dst[r:stop, :] = advance(src[r - 8 : stop + 8, :], fresh[t, r:stop, :], coef, shift)
        near[0:count, :] = dst[begin : begin + count, :]
        near[count:, :] = dst[end - count : end, :]
        for r in range(flat, ROWS - flat, 32):
            stop = min(r + 32, ROWS - flat)
            flats[t, r:stop, :] = dst[r:stop, :].astype(jnp.bfloat16)


def outer_kernel(
    wind,
    near0,
    fresh0,
    low,
    high,
    coef,
    near1,
    near2,
    near3,
    table,
    inside,
    old,
    images,
    screen_out,
    flat,
    piece,
    ends,
    sem,
):
    shift = wind[0] + 2
    none = jnp.zeros((8, COLS), jnp.float32)
    join = lambda *rows: jnp.concatenate(rows, axis=0)
    after = lambda window, fresh: advance(window, fresh, coef, shift)
    def project(t):
        for m in range(NM):
            image = lax.dot_general(
                table[m], flat[t], (((1,), (1,)), ((), ())), preferred_element_type=jnp.float32
            )
            for half in range(2):
                for part in range(2):
                    at = image[half * 256 : half * 256 + 256, part * LANES : part * LANES + LANES]
                    piece[t, :, part, m, half, :, :] = at.reshape(CHUNKS, 8, LANES)
        copy = pltpu.make_async_copy(piece.at[t], images.at[:, :, t], sem.at[t])
        copy.start()
        return copy

    first, final = fresh0[0, 0].astype(jnp.float32), fresh0[1, 0].astype(jnp.float32)
    e = after(join(low[0:16, :], near0[0]), join(low[16:24, :], first[0:8]))
    f = after(join(near0[1], high[0:16, :]), join(final[24:32], high[16:24, :]))
    flat[0] = inside[0]
    flat[0, 0:16, :] = join(e[8:16], near1[0:8, :]).astype(jnp.bfloat16)
    flat[0, ROWS - 16 : ROWS, :] = join(near1[24:32, :], f[0:8]).astype(jnp.bfloat16)
    leave = [project(0)]

    first, final = fresh0[0, 1].astype(jnp.float32), fresh0[1, 1].astype(jnp.float32)
    e = after(join(none, e, near1[0:16, :]), join(low[24:32, :], first[0:16]))
    f = after(join(near1[16:32, :], f, none), join(final[16:32], high[24:32, :]))
    flat[1] = inside[1]
    flat[1, 0:16, :] = e[8:24].astype(jnp.bfloat16)
    flat[1, ROWS - 16 : ROWS, :] = f[0:16].astype(jnp.bfloat16)
    leave.append(project(1))

    first, final = fresh0[0, 2].astype(jnp.float32), fresh0[1, 2].astype(jnp.float32)
    e = after(join(e, near2[0:16, :]), first[0:24])
    f = after(join(near2[16:32, :], f), final[8:32])
    ends[0] = e
    ends[1] = f
    leave += [
        pltpu.make_async_copy(ends.at[0], screen_out.at[pl.ds(0, 24), :], sem.at[3]),
        pltpu.make_async_copy(ends.at[1], screen_out.at[pl.ds(ROWS - 24, 24), :], sem.at[4]),
    ]
    leave[-2].start()
    leave[-1].start()
    flat[2] = inside[2]
    flat[2, 0:32, :] = join(e, near3[0:8, :]).astype(jnp.bfloat16)
    flat[2, ROWS - 32 : ROWS, :] = join(near3[8:16, :], f).astype(jnp.bfloat16)
    leave.append(project(2))
    for copy in leave:
        copy.wait()


def feet_kernel(places, x, feet):
    feet[...] = jnp.zeros(feet.shape, jnp.float32)
    lane = lax.broadcasted_iota(jnp.int32, (GROUP, LANES), 1)

    for layer in range(LAYERS):
        for d in range(NDIR):
            start = places[layer * 2 * NDIR + d]
            m = places[(layer * 2 + 1) * NDIR + d]
            block = start // 8
            shift = (start % 8) * 16
            back = (LANES - shift) % LANES
            rolled = []
            for i in range(5):
                rows = x[layer * 16 + (block + i) % 16, :, m]
                rolled.append(pltpu.roll(rows.reshape(GROUP, LANES), back, axis=1))
            for i in range(4):
                piece = jnp.where(lane < LANES - shift, rolled[i], rolled[i + 1])
                at = (m, pl.ds(d * GROUP, GROUP), pl.ds(i * LANES, LANES))
                feet[at] = feet[at] + piece


def pupil_kernel(mine, feet, table, *refs):
    *outs, pupils = refs
    total = None
    for m in range(NM):
        whole = feet[m]
        head = whole.astype(jnp.bfloat16)
        tail = (whole - head.astype(jnp.float32)).astype(jnp.bfloat16)
        for part in (head, tail):
            product = lax.dot_general(
                part, table[m], (((1,), (1,)), ((), ())), preferred_element_type=jnp.float32
            )
            total = product if total is None else total + product
    pupils[...] = total.reshape(pupils.shape)
    for out, parts in zip(outs, PARTS):
        for at, j in enumerate(parts):
            out[at * GROUP : at * GROUP + GROUP, :] = pupils[(mine[0] + j) % NDIR]


def pack_kernel(here, up1, down1, up2, down2, up3, out):
    total = here[...] + up1[...] + down1[...] + up2[...] + down2[...] + up3[...]
    tiles = [total[8 * j : 8 * j + 8] for j in range(6)]

    lane = lax.broadcasted_iota(jnp.int32, (8, LANES), 1)
    slot = lane // 16
    within = lane % 16
    heads = []
    for g in range(4):
        gathered = tiles[0][:, g * LANES : g * LANES + LANES]
        for j in range(1, 6):
            moved = pltpu.roll(tiles[j][:, g * LANES : g * LANES + LANES], j, axis=1)
            gathered = jnp.where(within == j, moved, gathered)
        heads.append(gathered)
    for g in range(4):
        for q in range(8):
            if q < 7:
                packed = pltpu.roll(heads[g], (96 - 16 * (q + 1)) % LANES, axis=1)
            elif g < 3:
                packed = pltpu.roll(heads[g + 1], 96, axis=1)
            else:
                packed = jnp.zeros((8, LANES), jnp.float32)
            for j in range(6):
                turn = (16 * j - 16 * q) % LANES
                moved = tiles[j][:, g * LANES : g * LANES + LANES]
                moved = moved if turn == 0 else pltpu.roll(moved, turn, axis=1)
                packed = jnp.where(slot == j, moved, packed)
            out[g * 8 + q] = packed


def slope_kernel(x, out):
    flipped = jnp.transpose(x[...].reshape(CHUNKS * 8, LANES))
    for t in range(STEPS):
        left = flipped[32 * t : 32 * t + 16]
        right = flipped[32 * t + 16 : 32 * t + 32]
        rows = jnp.concatenate([left, right], axis=1)
        edge = jnp.concatenate(
            [flipped[96 + 2 * t : 97 + 2 * t], flipped[97 + 2 * t : 98 + 2 * t]], axis=1
        )
        beside = jnp.concatenate([rows[:, 1:], jnp.zeros((16, 1), jnp.float32)], axis=1)
        below = jnp.concatenate([rows[1:], edge], axis=0)
        out[t, 0] = (beside - rows).reshape(16, 1, PC)
        out[t, 1] = (below - rows).reshape(16, 1, PC)


def neighbours(count, by):
    return [(i, (i + by) % count) for i in range(count)]


SCALARS = pl.BlockSpec(memory_space=pltpu.SMEM)


def room(mib):
    return pltpu.CompilerParams(vmem_limit_bytes=int(mib * 1024 * 1024))


def whole(*shape):
    return pl.BlockSpec(shape, lambda *_: (0,) * len(shape))


def shards(screen, innovation, coef, wind, row_blocks, table_index, row_table, column_table):
    state = screen[0]
    fresh = innovation[:, 0]
    strips = lax.axis_size("strip")

    near = jax.ShapeDtypeStruct((32, COLS), jnp.float32)
    taps = jax.ShapeDtypeStruct((TAPS, 1, COLS), jnp.float32)
    begin, last, state, fresh, taps = pl.pallas_call(
        ends_kernel,
        in_specs=[whole(ROWS, COLS), whole(STEPS, ROWS, COLS), whole(TAPS, 1, COLS)],
        out_specs=[
            whole(32, COLS),
            whole(32, COLS),
            whole(ROWS, COLS),
            whole(STEPS, ROWS, COLS),
            whole(TAPS, 1, COLS),
        ],
        out_shape=[
            near,
            near,
            jax.ShapeDtypeStruct((ROWS, COLS), jnp.float32),
            jax.ShapeDtypeStruct((STEPS, ROWS, COLS), jnp.bfloat16),
            taps,
        ],
        compiler_params=room(24),
        name="ends",
    )(state, fresh, jnp.swapaxes(coef, 0, 1))
    low = lax.ppermute(last, "strip", neighbours(strips, 1))
    high = lax.ppermute(begin, "strip", neighbours(strips, -1))

    *inside, unfinished = pl.pallas_call(
        inner_kernel,
        in_specs=[
            SCALARS,
            whole(ROWS, COLS),
            whole(STEPS, ROWS, COLS),
            whole(TAPS, 1, COLS),
        ],
        out_specs=[
            whole(STEPS, ROWS, COLS),
            whole(2, 16, COLS),
            whole(2, STEPS, 32, COLS),
            whole(32, COLS),
            whole(32, COLS),
            whole(16, COLS),
            whole(ROWS, COLS),
        ],
        out_shape=[
            jax.ShapeDtypeStruct((STEPS, ROWS, COLS), jnp.bfloat16),
            jax.ShapeDtypeStruct((2, 16, COLS), jnp.float32),
            jax.ShapeDtypeStruct((2, STEPS, 32, COLS), jnp.bfloat16),
            near,
            near,
            jax.ShapeDtypeStruct((16, COLS), jnp.float32),
            jax.ShapeDtypeStruct((ROWS, COLS), jnp.float32),
        ],
        scratch_shapes=[pltpu.VMEM((ROWS, COLS), jnp.float32)] * 2,
        compiler_params=room(24),
        cost_estimate=pl.CostEstimate(
            flops=12 * STEPS * ROWS * COLS, bytes_accessed=100 * ROWS * COLS, transcendentals=0
        ),
        name="inner",
    )(wind, state, fresh, taps)

    anywhere = pl.BlockSpec(memory_space=pl.ANY)
    images, screen_out = pl.pallas_call(
        outer_kernel,
        in_specs=[
            SCALARS,
            whole(2, 16, COLS),
            whole(2, STEPS, 32, COLS),
            whole(32, COLS),
            whole(32, COLS),
            whole(TAPS, 1, COLS),
            whole(32, COLS),
            whole(32, COLS),
            whole(16, COLS),
            whole(NM, PC, COLS),
            whole(STEPS, ROWS, COLS),
            anywhere,
        ],
        out_specs=[anywhere, anywhere],
        out_shape=[
            jax.ShapeDtypeStruct((CHUNKS, 2, STEPS, NM, 2, 8, LANES), jnp.float32),
            jax.ShapeDtypeStruct((ROWS, COLS), jnp.float32),
        ],
        input_output_aliases={11: 1},
        scratch_shapes=[
            pltpu.VMEM((STEPS, ROWS, COLS), jnp.bfloat16),
            pltpu.VMEM((STEPS, CHUNKS, 2, NM, 2, 8, LANES), jnp.float32),
            pltpu.VMEM((2, 24, COLS), jnp.float32),
            pltpu.SemaphoreType.DMA((5,)),
        ],
        compiler_params=room(50),
        name="outer",
    )(
        wind,
        *inside[1:3],
        low,
        high,
        taps,
        *inside[3:6],
        column_table,
        inside[0],
        unfinished,
    )

    gathered = lax.all_to_all(images, PLANE, 0, 0, tiled=True)
    places = jnp.stack([row_blocks[:, 0, 0], table_index[:, 0]])
    places = lax.all_gather(places, "layer").reshape(LAYERS * 2 * NDIR)
    mine = lax.axis_index("dir").astype(jnp.int32).reshape(1)
    feet = pl.pallas_call(
        feet_kernel,
        in_specs=[SCALARS, whole(CHUNKS * 2, STEPS, NM, 2, 8, LANES)],
        out_specs=whole(NM, NDIR * GROUP, PR),
        out_shape=jax.ShapeDtypeStruct((NM, NDIR * GROUP, PR), jnp.float32),
        compiler_params=room(24),
        cost_estimate=pl.CostEstimate(flops=0, bytes_accessed=100 * ROWS * COLS, transcendentals=0),
        name="feet",
    )(places, gathered.reshape(CHUNKS * 2, STEPS, NM, 2, 8, LANES))
    pupils = pl.pallas_call(
        pupil_kernel,
        in_specs=[SCALARS, whole(NM, NDIR * GROUP, PR), whole(NM, PR, PR)],
        out_specs=[whole(len(parts) * GROUP, PR) for parts in PARTS],
        out_shape=[jax.ShapeDtypeStruct((len(parts) * GROUP, PR), jnp.float32) for parts in PARTS],
        scratch_shapes=[pltpu.VMEM((NDIR, GROUP, PR), jnp.float32)],
        compiler_params=room(24),
        name="pupil",
    )(mine, feet, row_table)

    count = lax.axis_size("dir")
    send = lambda x, by: lax.ppermute(x, "dir", neighbours(count, by))
    far = send(pupils[4], -2)
    up3 = send(pupils[3], 3)
    down3 = send(pupils[5], -1)
    up2 = send(pupils[2], 2)
    down1 = send(pupils[7], -1)
    up1 = send(pupils[1], 1)
    down2 = send(pupils[6] + down3 + far, -2)
    terms = [pupils[0], up1, down1, up2, down2, up3]

    packed = pl.pallas_call(
        pack_kernel,
        in_specs=[whole(GROUP, PR)] * 6,
        out_specs=whole(CHUNKS, 8, LANES),
        out_shape=jax.ShapeDtypeStruct((CHUNKS, 8, LANES), jnp.float32),
        compiler_params=room(16),
        name="pack",
    )(*terms)
    rows = lax.all_to_all(packed, PLANE, 0, 0, tiled=True)
    slopes = pl.pallas_call(
        slope_kernel,
        in_specs=[whole(CHUNKS, 8, LANES)],
        out_specs=whole(STEPS, 2, 16, 1, PC),
        out_shape=jax.ShapeDtypeStruct((STEPS, 2, 16, 1, PC), jnp.float32),
        compiler_params=room(16),
        name="slopes",
    )(rows)
    return (screen_out[None], slopes)


def solution(mesh):
    return jax.shard_map(
        shards,
        mesh=mesh,
        in_specs=(
            P("layer", "strip", "dir"),
            P(None, "layer", "strip", "dir"),
            P("layer", None, "dir"),
            P("layer"),
            P(None, "layer", None),
            P(None, "layer"),
            P(),
            P(None, None, "dir"),
        ),
        out_specs=(P("layer", "strip", "dir"), P(None, None, ("layer", "strip"), "dir", None)),
        check_vma=False,
    )
```

```python
import jax
import jax.numpy as jnp
from jax import lax
from jax.experimental import pallas as pl
from jax.experimental.pallas import tpu as pltpu
from jax.sharding import PartitionSpec as P

ROWS = 256
COLS = 512
PR = 512
PC = 512
STEPS = 3
NM = 2
NDIR = 8
LAYERS = 4
STRIPS = 8
TAPS = 5
CHUNKS = LAYERS * STRIPS
PAD = 16
LANES = 128
GROUP = STEPS * 2 * 8
PLANE = ("layer", "strip")
PARTS = ((0,), (1,), (2,), (3,), (4,), (5,), (6,), (7,))


def advance(window, fresh, coef, shift):
    count = fresh.shape[0]
    moved = pltpu.roll(window, shift, axis=0)
    total = fresh.astype(jnp.float32)
    for k in range(TAPS):
        total = total + coef[k] * moved[8 + k : 8 + k + count, :]
    return total


def ends_kernel(screen, fresh, begin, last, screen_on, fresh_on):
    begin[0:16, :] = screen[0:16, :]
    last[0:16, :] = screen[ROWS - 16 : ROWS, :]
    for t in range(2):
        at = slice(16 + 8 * t, 24 + 8 * t)
        begin[at, :] = fresh[t, 0:16, :].astype(jnp.float32)[0:8, :]
        last[at, :] = fresh[t, ROWS - 16 : ROWS, :].astype(jnp.float32)[8:16, :]
    screen_on[...] = screen[...]
    fresh_on[...] = fresh[...]


def inner_kernel(
    wind, screen, fresh, coef, flats, near0, fresh0, near1, near2, near3, coef_on, s3, s1, s2
):
    shift = wind[0] + 2
    coef_on[...] = coef[...]
    near0[0] = screen[0:16, :]
    near0[1] = screen[ROWS - 16 : ROWS, :]
    fresh0[0] = fresh[:, 0:32, :]
    fresh0[1] = fresh[:, ROWS - 32 : ROWS, :]
    steps = ((screen, s1, near1, 16, 16), (s1, s2, near2, 16, 16), (s2, s3, near3, 8, 32))
    for t, (src, dst, near, count, flat) in enumerate(steps):
        begin, end = 8 * (t + 1), ROWS - 8 * (t + 1)
        for r in range(begin, end, 64):
            stop = min(r + 64, end)
            for c in range(0, COLS, LANES):
                at = slice(c, c + LANES)
                dst[r:stop, at] = advance(
                    src[r - 8 : stop + 8, at], fresh[t, r:stop, at], coef[:, :, at], shift
                )
        near[0:count, :] = dst[begin : begin + count, :]
        near[count:, :] = dst[end - count : end, :]
        for r in range(flat, ROWS - flat, 32):
            stop = min(r + 32, ROWS - flat)
            flats[t, r:stop, :] = dst[r:stop, :].astype(jnp.bfloat16)


def outer_kernel(
    wind,
    near0,
    fresh0,
    low,
    high,
    coef,
    near1,
    near2,
    near3,
    table,
    inside,
    old,
    images,
    screen_out,
    flat,
    piece,
    ends,
    sem,
):
    shift = wind[0] + 2
    none = jnp.zeros((8, COLS), jnp.float32)
    join = lambda *rows: jnp.concatenate(rows, axis=0)
    after = lambda window, fresh: advance(window, fresh, coef, shift)
    leave = []

    def project(t):
        for m in range(NM):
            image = lax.dot_general(
                table[m], flat[t], (((1,), (1,)), ((), ())), preferred_element_type=jnp.float32
            )
            for half in range(2):
                for part in range(2):
                    at = image[half * 256 : half * 256 + 256, part * LANES : part * LANES + LANES]
                    piece[t, m, :, part, half, :, :] = at.reshape(CHUNKS, 8, LANES)
            copy = pltpu.make_async_copy(piece.at[t, m], images.at[:, :, t, m], sem.at[NM * t + m])
            copy.start()
            leave.append(copy)

    first, final = fresh0[0, 0].astype(jnp.float32), fresh0[1, 0].astype(jnp.float32)
    e = after(join(low[0:16, :], near0[0]), join(low[16:24, :], first[0:8]))
    f = after(join(near0[1], high[0:16, :]), join(final[24:32], high[16:24, :]))
    flat[0] = inside[0]
    flat[0, 0:16, :] = join(e[8:16], near1[0:8, :]).astype(jnp.bfloat16)
    flat[0, ROWS - 16 : ROWS, :] = join(near1[24:32, :], f[0:8]).astype(jnp.bfloat16)
    project(0)

    first, final = fresh0[0, 1].astype(jnp.float32), fresh0[1, 1].astype(jnp.float32)
    e = after(join(none, e, near1[0:16, :]), join(low[24:32, :], first[0:16]))
    f = after(join(near1[16:32, :], f, none), join(final[16:32], high[24:32, :]))
    flat[1] = inside[1]
    flat[1, 0:16, :] = e[8:24].astype(jnp.bfloat16)
    flat[1, ROWS - 16 : ROWS, :] = f[0:16].astype(jnp.bfloat16)
    project(1)

    first, final = fresh0[0, 2].astype(jnp.float32), fresh0[1, 2].astype(jnp.float32)
    e = after(join(e, near2[0:16, :]), first[0:24])
    f = after(join(near2[16:32, :], f), final[8:32])
    ends[0] = e
    ends[1] = f
    leave += [
        pltpu.make_async_copy(ends.at[0], screen_out.at[pl.ds(0, 24), :], sem.at[6]),
        pltpu.make_async_copy(ends.at[1], screen_out.at[pl.ds(ROWS - 24, 24), :], sem.at[7]),
    ]
    leave[-2].start()
    leave[-1].start()
    flat[2] = inside[2]
    flat[2, 0:32, :] = join(e, near3[0:8, :]).astype(jnp.bfloat16)
    flat[2, ROWS - 32 : ROWS, :] = join(near3[8:16, :], f).astype(jnp.bfloat16)
    project(2)
    for copy in leave:
        copy.wait()


def feet_kernel(places, x, feet):
    feet[...] = jnp.zeros(feet.shape, jnp.float32)
    lane = lax.broadcasted_iota(jnp.int32, (GROUP, LANES), 1)

    for layer in range(LAYERS):
        for d in range(NDIR):
            start = places[layer * 2 * NDIR + d]
            m = places[(layer * 2 + 1) * NDIR + d]
            block = start // 8
            shift = (start % 8) * 16
            back = (LANES - shift) % LANES
            rolled = []
            for i in range(5):
                rows = x[layer * 16 + (block + i) % 16, :, m]
                rolled.append(pltpu.roll(rows.reshape(GROUP, LANES), back, axis=1))
            for i in range(4):
                piece = jnp.where(lane < LANES - shift, rolled[i], rolled[i + 1])
                at = (m, pl.ds(d * GROUP, GROUP), pl.ds(i * LANES, LANES))
                feet[at] = feet[at] + piece


def pupil_kernel(mine, feet, table, *refs):
    *outs, pupils = refs
    total = None
    for m in range(NM):
        whole = feet[m]
        head = whole.astype(jnp.bfloat16)
        tail = (whole - head.astype(jnp.float32)).astype(jnp.bfloat16)
        for part in (head, tail):
            product = lax.dot_general(
                part, table[m], (((1,), (1,)), ((), ())), preferred_element_type=jnp.float32
            )
            total = product if total is None else total + product
    pupils[...] = total.reshape(pupils.shape)
    for out, parts in zip(outs, PARTS):
        for at, j in enumerate(parts):
            out[at * GROUP : at * GROUP + GROUP, :] = pupils[(mine[0] + j) % NDIR]


def pack_kernel(here, up1, down1, up2, down2, up3, out):
    total = here[...] + up1[...] + down1[...] + up2[...] + down2[...] + up3[...]
    tiles = [total[8 * j : 8 * j + 8] for j in range(6)]

    lane = lax.broadcasted_iota(jnp.int32, (8, LANES), 1)
    slot = lane // 16
    within = lane % 16
    heads = []
    for g in range(4):
        gathered = tiles[0][:, g * LANES : g * LANES + LANES]
        for j in range(1, 6):
            moved = pltpu.roll(tiles[j][:, g * LANES : g * LANES + LANES], j, axis=1)
            gathered = jnp.where(within == j, moved, gathered)
        heads.append(gathered)
    for g in range(4):
        for q in range(8):
            if q < 7:
                packed = pltpu.roll(heads[g], (96 - 16 * (q + 1)) % LANES, axis=1)
            elif g < 3:
                packed = pltpu.roll(heads[g + 1], 96, axis=1)
            else:
                packed = jnp.zeros((8, LANES), jnp.float32)
            for j in range(6):
                turn = (16 * j - 16 * q) % LANES
                moved = tiles[j][:, g * LANES : g * LANES + LANES]
                moved = moved if turn == 0 else pltpu.roll(moved, turn, axis=1)
                packed = jnp.where(slot == j, moved, packed)
            out[g * 8 + q] = packed


def slope_kernel(x, out):
    flipped = jnp.transpose(x[...].reshape(CHUNKS * 8, LANES))
    for t in range(STEPS):
        left = flipped[32 * t : 32 * t + 16]
        right = flipped[32 * t + 16 : 32 * t + 32]
        rows = jnp.concatenate([left, right], axis=1)
        edge = jnp.concatenate(
            [flipped[96 + 2 * t : 97 + 2 * t], flipped[97 + 2 * t : 98 + 2 * t]], axis=1
        )
        beside = jnp.concatenate([rows[:, 1:], jnp.zeros((16, 1), jnp.float32)], axis=1)
        below = jnp.concatenate([rows[1:], edge], axis=0)
        out[t, 0] = (beside - rows).reshape(16, 1, PC)
        out[t, 1] = (below - rows).reshape(16, 1, PC)


def neighbours(count, by):
    return [(i, (i + by) % count) for i in range(count)]


SCALARS = pl.BlockSpec(memory_space=pltpu.SMEM)


def room(mib):
    return pltpu.CompilerParams(vmem_limit_bytes=int(mib * 1024 * 1024))


def whole(*shape):
    return pl.BlockSpec(shape, lambda *_: (0,) * len(shape))


def shards(screen, innovation, coef, wind, row_blocks, table_index, row_table, column_table):
    state = screen[0]
    fresh = innovation[:, 0]
    strips = lax.axis_size("strip")

    near = jax.ShapeDtypeStruct((32, COLS), jnp.float32)
    taps = jax.ShapeDtypeStruct((TAPS, 1, COLS), jnp.float32)
    begin, last, state, fresh = pl.pallas_call(
        ends_kernel,
        in_specs=[whole(ROWS, COLS), whole(STEPS, ROWS, COLS)],
        out_specs=[
            whole(32, COLS),
            whole(32, COLS),
            whole(ROWS, COLS),
            whole(STEPS, ROWS, COLS),
        ],
        out_shape=[
            near,
            near,
            jax.ShapeDtypeStruct((ROWS, COLS), jnp.float32),
            jax.ShapeDtypeStruct((STEPS, ROWS, COLS), jnp.bfloat16),
        ],
        compiler_params=room(24),
        name="ends",
    )(state, fresh)
    low = lax.ppermute(last, "strip", neighbours(strips, 1))
    high = lax.ppermute(begin, "strip", neighbours(strips, -1))

    *inside, unfinished = pl.pallas_call(
        inner_kernel,
        in_specs=[
            SCALARS,
            whole(ROWS, COLS),
            whole(STEPS, ROWS, COLS),
            whole(TAPS, 1, COLS),
        ],
        out_specs=[
            whole(STEPS, ROWS, COLS),
            whole(2, 16, COLS),
            whole(2, STEPS, 32, COLS),
            whole(32, COLS),
            whole(32, COLS),
            whole(16, COLS),
            whole(TAPS, 1, COLS),
            whole(ROWS, COLS),
        ],
        out_shape=[
            jax.ShapeDtypeStruct((STEPS, ROWS, COLS), jnp.bfloat16),
            jax.ShapeDtypeStruct((2, 16, COLS), jnp.float32),
            jax.ShapeDtypeStruct((2, STEPS, 32, COLS), jnp.bfloat16),
            near,
            near,
            jax.ShapeDtypeStruct((16, COLS), jnp.float32),
            taps,
            jax.ShapeDtypeStruct((ROWS, COLS), jnp.float32),
        ],
        scratch_shapes=[pltpu.VMEM((ROWS, COLS), jnp.float32)] * 2,
        compiler_params=room(24),
        cost_estimate=pl.CostEstimate(
            flops=12 * STEPS * ROWS * COLS, bytes_accessed=100 * ROWS * COLS, transcendentals=0
        ),
        name="inner",
    )(wind, state, fresh, jnp.swapaxes(coef, 0, 1))

    anywhere = pl.BlockSpec(memory_space=pl.ANY)
    images, screen_out = pl.pallas_call(
        outer_kernel,
        in_specs=[
            SCALARS,
            whole(2, 16, COLS),
            whole(2, STEPS, 32, COLS),
            whole(32, COLS),
            whole(32, COLS),
            whole(TAPS, 1, COLS),
            whole(32, COLS),
            whole(32, COLS),
            whole(16, COLS),
            whole(NM, PC, COLS),
            whole(STEPS, ROWS, COLS),
            anywhere,
        ],
        out_specs=[anywhere, anywhere],
        out_shape=[
            jax.ShapeDtypeStruct((CHUNKS, 2, STEPS, NM, 2, 8, LANES), jnp.float32),
            jax.ShapeDtypeStruct((ROWS, COLS), jnp.float32),
        ],
        input_output_aliases={11: 1},
        scratch_shapes=[
            pltpu.VMEM((STEPS, ROWS, COLS), jnp.bfloat16),
            pltpu.VMEM((STEPS, NM, CHUNKS, 2, 2, 8, LANES), jnp.float32),
            pltpu.VMEM((2, 24, COLS), jnp.float32),
            pltpu.SemaphoreType.DMA((8,)),
        ],
        compiler_params=room(50),
        name="outer",
    )(
        wind,
        *inside[1:3],
        low,
        high,
        inside[6],
        *inside[3:6],
        column_table,
        inside[0],
        unfinished,
    )

    gathered = lax.all_to_all(images, PLANE, 0, 0, tiled=True)
    places = jnp.stack([row_blocks[:, 0, 0], table_index[:, 0]])
    places = lax.all_gather(places, "layer").reshape(LAYERS * 2 * NDIR)
    mine = lax.axis_index("dir").astype(jnp.int32).reshape(1)
    feet = pl.pallas_call(
        feet_kernel,
        in_specs=[SCALARS, whole(CHUNKS * 2, STEPS, NM, 2, 8, LANES)],
        out_specs=whole(NM, NDIR * GROUP, PR),
        out_shape=jax.ShapeDtypeStruct((NM, NDIR * GROUP, PR), jnp.float32),
        compiler_params=room(24),
        cost_estimate=pl.CostEstimate(flops=0, bytes_accessed=100 * ROWS * COLS, transcendentals=0),
        name="feet",
    )(places, gathered.reshape(CHUNKS * 2, STEPS, NM, 2, 8, LANES))
    pupils = pl.pallas_call(
        pupil_kernel,
        in_specs=[SCALARS, whole(NM, NDIR * GROUP, PR), whole(NM, PR, PR)],
        out_specs=[whole(len(parts) * GROUP, PR) for parts in PARTS],
        out_shape=[jax.ShapeDtypeStruct((len(parts) * GROUP, PR), jnp.float32) for parts in PARTS],
        scratch_shapes=[pltpu.VMEM((NDIR, GROUP, PR), jnp.float32)],
        compiler_params=room(24),
        name="pupil",
    )(mine, feet, row_table)

    count = lax.axis_size("dir")
    send = lambda x, by: lax.ppermute(x, "dir", neighbours(count, by))
    far = send(pupils[4], -2)
    down3 = send(pupils[5], -2)
    up3 = send(pupils[3], 3)
    up2 = send(pupils[2], 2)
    up1 = send(pupils[1], 1)
    down2 = send(pupils[6] + far, -2)
    down1 = send(pupils[7] + down3, -1)
    terms = [pupils[0], up1, down1, up2, down2, up3]

    packed = pl.pallas_call(
        pack_kernel,
        in_specs=[whole(GROUP, PR)] * 6,
        out_specs=whole(CHUNKS, 8, LANES),
        out_shape=jax.ShapeDtypeStruct((CHUNKS, 8, LANES), jnp.float32),
        compiler_params=room(16),
        name="pack",
    )(*terms)
    rows = lax.all_to_all(packed, PLANE, 0, 0, tiled=True)
    slopes = pl.pallas_call(
        slope_kernel,
        in_specs=[whole(CHUNKS, 8, LANES)],
        out_specs=whole(STEPS, 2, 16, 1, PC),
        out_shape=jax.ShapeDtypeStruct((STEPS, 2, 16, 1, PC), jnp.float32),
        compiler_params=room(16),
        name="slopes",
    )(rows)
    return (screen_out[None], slopes)


def solution(mesh):
    return jax.shard_map(
        shards,
        mesh=mesh,
        in_specs=(
            P("layer", "strip", "dir"),
            P(None, "layer", "strip", "dir"),
            P("layer", None, "dir"),
            P("layer"),
            P(None, "layer", None),
            P(None, "layer"),
            P(),
            P(None, None, "dir"),
        ),
        out_specs=(P("layer", "strip", "dir"), P(None, None, ("layer", "strip"), "dir", None)),
        check_vma=False,
    )
```

```python
import jax
import jax.numpy as jnp
from jax import lax
from jax.experimental import pallas as pl
from jax.experimental.pallas import tpu as pltpu
from jax.sharding import PartitionSpec as P

ROWS = 256
COLS = 512
PR = 512
PC = 512
STEPS = 3
NM = 2
NDIR = 8
LAYERS = 4
STRIPS = 8
TAPS = 5
CHUNKS = LAYERS * STRIPS
PAD = 16
LANES = 128
GROUP = STEPS * 2 * 8
PLANE = ("layer", "strip")
PARTS = ((0,), (1,), (2,), (3,), (4,), (5,), (6,), (7,))


def advance(window, fresh, coef, shift):
    count = fresh.shape[0]
    moved = pltpu.roll(window, shift, axis=0)
    total = fresh.astype(jnp.float32)
    for k in range(TAPS):
        total = total + coef[k] * moved[8 + k : 8 + k + count, :]
    return total


def ends_kernel(screen, fresh, begin, last, screen_on, fresh_on):
    begin[0:16, :] = screen[0:16, :]
    last[0:16, :] = screen[ROWS - 16 : ROWS, :]
    for t in range(2):
        at = slice(16 + 8 * t, 24 + 8 * t)
        begin[at, :] = fresh[t, 0:16, :].astype(jnp.float32)[0:8, :]
        last[at, :] = fresh[t, ROWS - 16 : ROWS, :].astype(jnp.float32)[8:16, :]
    screen_on[...] = screen[...]
    fresh_on[...] = fresh[...]


def inner_kernel(
    wind, screen, fresh, coef, flats, near0, fresh0, near1, near2, near3, coef_on, s3, s1, s2
):
    shift = wind[0] + 2
    coef_on[...] = coef[...]
    near0[0] = screen[0:16, :]
    near0[1] = screen[ROWS - 16 : ROWS, :]
    fresh0[0] = fresh[:, 0:32, :]
    fresh0[1] = fresh[:, ROWS - 32 : ROWS, :]
    steps = ((screen, s1, near1, 16, 16), (s1, s2, near2, 16, 16), (s2, s3, near3, 8, 32))
    for t, (src, dst, near, count, flat) in enumerate(steps):
        begin, end = 8 * (t + 1), ROWS - 8 * (t + 1)
        for r in range(begin, end, 64):
            stop = min(r + 64, end)
            for c in range(0, COLS, LANES):
                at = slice(c, c + LANES)
                low, high = r // 16 * 16, -(-stop // 16) * 16
                rows = fresh[t, low:high, at].astype(jnp.float32)[r - low : stop - low]
                dst[r:stop, at] = advance(
                    src[r - 8 : stop + 8, at], rows, coef[:, :, at], shift
                )
        near[0:count, :] = dst[begin : begin + count, :]
        near[count:, :] = dst[end - count : end, :]
        for r in range(flat, ROWS - flat, 32):
            stop = min(r + 32, ROWS - flat)
            flats[t, r:stop, :] = dst[r:stop, :].astype(jnp.bfloat16)


def outer_kernel(
    wind,
    near0,
    fresh0,
    low,
    high,
    coef,
    near1,
    near2,
    near3,
    table,
    inside,
    old,
    images,
    screen_out,
    flat,
    piece,
    ends,
    sem,
):
    shift = wind[0] + 2
    none = jnp.zeros((8, COLS), jnp.float32)
    join = lambda *rows: jnp.concatenate(rows, axis=0)
    after = lambda window, fresh: advance(window, fresh, coef, shift)
    leave = []

    def project(t):
        for m in range(NM):
            image = lax.dot_general(
                table[m], flat[t], (((1,), (1,)), ((), ())), preferred_element_type=jnp.float32
            )
            for half in range(2):
                for part in range(2):
                    at = image[half * 256 : half * 256 + 256, part * LANES : part * LANES + LANES]
                    piece[t, m, :, part, half, :, :] = at.reshape(CHUNKS, 8, LANES)
            copy = pltpu.make_async_copy(piece.at[t, m], images.at[:, :, t, m], sem.at[NM * t + m])
            copy.start()
            leave.append(copy)

    first, final = fresh0[0, 0].astype(jnp.float32), fresh0[1, 0].astype(jnp.float32)
    e = after(join(low[0:16, :], near0[0]), join(low[16:24, :], first[0:8]))
    f = after(join(near0[1], high[0:16, :]), join(final[24:32], high[16:24, :]))
    flat[0] = inside[0]
    flat[0, 0:16, :] = join(e[8:16], near1[0:8, :]).astype(jnp.bfloat16)
    flat[0, ROWS - 16 : ROWS, :] = join(near1[24:32, :], f[0:8]).astype(jnp.bfloat16)
    project(0)

    first, final = fresh0[0, 1].astype(jnp.float32), fresh0[1, 1].astype(jnp.float32)
    e = after(join(none, e, near1[0:16, :]), join(low[24:32, :], first[0:16]))
    f = after(join(near1[16:32, :], f, none), join(final[16:32], high[24:32, :]))
    flat[1] = inside[1]
    flat[1, 0:16, :] = e[8:24].astype(jnp.bfloat16)
    flat[1, ROWS - 16 : ROWS, :] = f[0:16].astype(jnp.bfloat16)
    project(1)

    first, final = fresh0[0, 2].astype(jnp.float32), fresh0[1, 2].astype(jnp.float32)
    e = after(join(e, near2[0:16, :]), first[0:24])
    f = after(join(near2[16:32, :], f), final[8:32])
    ends[0] = e
    ends[1] = f
    leave += [
        pltpu.make_async_copy(ends.at[0], screen_out.at[pl.ds(0, 24), :], sem.at[6]),
        pltpu.make_async_copy(ends.at[1], screen_out.at[pl.ds(ROWS - 24, 24), :], sem.at[7]),
    ]
    leave[-2].start()
    leave[-1].start()
    flat[2] = inside[2]
    flat[2, 0:32, :] = join(e, near3[0:8, :]).astype(jnp.bfloat16)
    flat[2, ROWS - 32 : ROWS, :] = join(near3[8:16, :], f).astype(jnp.bfloat16)
    project(2)
    for copy in leave:
        copy.wait()


def feet_kernel(places, x, feet):
    feet[...] = jnp.zeros(feet.shape, jnp.float32)
    lane = lax.broadcasted_iota(jnp.int32, (GROUP, LANES), 1)

    for layer in range(LAYERS):
        for d in range(NDIR):
            start = places[layer * 2 * NDIR + d]
            m = places[(layer * 2 + 1) * NDIR + d]
            block = start // 8
            shift = (start % 8) * 16
            back = (LANES - shift) % LANES
            rolled = []
            for i in range(5):
                rows = x[layer * 16 + (block + i) % 16, :, m]
                rolled.append(pltpu.roll(rows.reshape(GROUP, LANES), back, axis=1))
            for i in range(4):
                piece = jnp.where(lane < LANES - shift, rolled[i], rolled[i + 1])
                at = (m, pl.ds(d * GROUP, GROUP), pl.ds(i * LANES, LANES))
                feet[at] = feet[at] + piece


def pupil_kernel(mine, feet, table, *refs):
    *outs, pupils = refs
    total = None
    for m in range(NM):
        whole = feet[m]
        head = whole.astype(jnp.bfloat16)
        tail = (whole - head.astype(jnp.float32)).astype(jnp.bfloat16)
        for part in (head, tail):
            product = lax.dot_general(
                part, table[m], (((1,), (1,)), ((), ())), preferred_element_type=jnp.float32
            )
            total = product if total is None else total + product
    pupils[...] = total.reshape(pupils.shape)
    for out, parts in zip(outs, PARTS):
        for at, j in enumerate(parts):
            out[at * GROUP : at * GROUP + GROUP, :] = pupils[(mine[0] + j) % NDIR]


def pack_kernel(here, up1, down1, up2, down2, up3, out):
    total = here[...] + up1[...] + down1[...] + up2[...] + down2[...] + up3[...]
    tiles = [total[8 * j : 8 * j + 8] for j in range(6)]

    lane = lax.broadcasted_iota(jnp.int32, (8, LANES), 1)
    slot = lane // 16
    within = lane % 16
    heads = []
    for g in range(4):
        gathered = tiles[0][:, g * LANES : g * LANES + LANES]
        for j in range(1, 6):
            moved = pltpu.roll(tiles[j][:, g * LANES : g * LANES + LANES], j, axis=1)
            gathered = jnp.where(within == j, moved, gathered)
        heads.append(gathered)
    for g in range(4):
        for q in range(8):
            if q < 7:
                packed = pltpu.roll(heads[g], (96 - 16 * (q + 1)) % LANES, axis=1)
            elif g < 3:
                packed = pltpu.roll(heads[g + 1], 96, axis=1)
            else:
                packed = jnp.zeros((8, LANES), jnp.float32)
            for j in range(6):
                turn = (16 * j - 16 * q) % LANES
                moved = tiles[j][:, g * LANES : g * LANES + LANES]
                moved = moved if turn == 0 else pltpu.roll(moved, turn, axis=1)
                packed = jnp.where(slot == j, moved, packed)
            out[g * 8 + q] = packed


def slope_kernel(x, out):
    flipped = jnp.transpose(x[...].reshape(CHUNKS * 8, LANES))
    for t in range(STEPS):
        left = flipped[32 * t : 32 * t + 16]
        right = flipped[32 * t + 16 : 32 * t + 32]
        rows = jnp.concatenate([left, right], axis=1)
        edge = jnp.concatenate(
            [flipped[96 + 2 * t : 97 + 2 * t], flipped[97 + 2 * t : 98 + 2 * t]], axis=1
        )
        beside = jnp.concatenate([rows[:, 1:], jnp.zeros((16, 1), jnp.float32)], axis=1)
        below = jnp.concatenate([rows[1:], edge], axis=0)
        out[t, 0] = (beside - rows).reshape(16, 1, PC)
        out[t, 1] = (below - rows).reshape(16, 1, PC)


def neighbours(count, by):
    return [(i, (i + by) % count) for i in range(count)]


SCALARS = pl.BlockSpec(memory_space=pltpu.SMEM)


def room(mib):
    return pltpu.CompilerParams(vmem_limit_bytes=int(mib * 1024 * 1024))


def whole(*shape):
    return pl.BlockSpec(shape, lambda *_: (0,) * len(shape))


def shards(screen, innovation, coef, wind, row_blocks, table_index, row_table, column_table):
    state = screen[0]
    fresh = innovation[:, 0]
    strips = lax.axis_size("strip")

    near = jax.ShapeDtypeStruct((32, COLS), jnp.float32)
    taps = jax.ShapeDtypeStruct((TAPS, 1, COLS), jnp.float32)
    begin, last, state, fresh = pl.pallas_call(
        ends_kernel,
        in_specs=[whole(ROWS, COLS), whole(STEPS, ROWS, COLS)],
        out_specs=[
            whole(32, COLS),
            whole(32, COLS),
            whole(ROWS, COLS),
            whole(STEPS, ROWS, COLS),
        ],
        out_shape=[
            near,
            near,
            jax.ShapeDtypeStruct((ROWS, COLS), jnp.float32),
            jax.ShapeDtypeStruct((STEPS, ROWS, COLS), jnp.bfloat16),
        ],
        compiler_params=room(24),
        name="ends",
    )(state, fresh)
    low = lax.ppermute(last, "strip", neighbours(strips, 1))
    high = lax.ppermute(begin, "strip", neighbours(strips, -1))

    *inside, unfinished = pl.pallas_call(
        inner_kernel,
        in_specs=[
            SCALARS,
            whole(ROWS, COLS),
            whole(STEPS, ROWS, COLS),
            whole(TAPS, 1, COLS),
        ],
        out_specs=[
            whole(STEPS, ROWS, COLS),
            whole(2, 16, COLS),
            whole(2, STEPS, 32, COLS),
            whole(32, COLS),
            whole(32, COLS),
            whole(16, COLS),
            whole(TAPS, 1, COLS),
            whole(ROWS, COLS),
        ],
        out_shape=[
            jax.ShapeDtypeStruct((STEPS, ROWS, COLS), jnp.bfloat16),
            jax.ShapeDtypeStruct((2, 16, COLS), jnp.float32),
            jax.ShapeDtypeStruct((2, STEPS, 32, COLS), jnp.bfloat16),
            near,
            near,
            jax.ShapeDtypeStruct((16, COLS), jnp.float32),
            taps,
            jax.ShapeDtypeStruct((ROWS, COLS), jnp.float32),
        ],
        scratch_shapes=[pltpu.VMEM((ROWS, COLS), jnp.float32)] * 2,
        compiler_params=room(24),
        cost_estimate=pl.CostEstimate(
            flops=12 * STEPS * ROWS * COLS, bytes_accessed=100 * ROWS * COLS, transcendentals=0
        ),
        name="inner",
    )(wind, state, fresh, jnp.swapaxes(coef, 0, 1))

    anywhere = pl.BlockSpec(memory_space=pl.ANY)
    images, screen_out = pl.pallas_call(
        outer_kernel,
        in_specs=[
            SCALARS,
            whole(2, 16, COLS),
            whole(2, STEPS, 32, COLS),
            whole(32, COLS),
            whole(32, COLS),
            whole(TAPS, 1, COLS),
            whole(32, COLS),
            whole(32, COLS),
            whole(16, COLS),
            whole(NM, PC, COLS),
            whole(STEPS, ROWS, COLS),
            anywhere,
        ],
        out_specs=[anywhere, anywhere],
        out_shape=[
            jax.ShapeDtypeStruct((CHUNKS, 2, STEPS, NM, 2, 8, LANES), jnp.float32),
            jax.ShapeDtypeStruct((ROWS, COLS), jnp.float32),
        ],
        input_output_aliases={11: 1},
        scratch_shapes=[
            pltpu.VMEM((STEPS, ROWS, COLS), jnp.bfloat16),
            pltpu.VMEM((STEPS, NM, CHUNKS, 2, 2, 8, LANES), jnp.float32),
            pltpu.VMEM((2, 24, COLS), jnp.float32),
            pltpu.SemaphoreType.DMA((8,)),
        ],
        compiler_params=room(50),
        name="outer",
    )(
        wind,
        *inside[1:3],
        low,
        high,
        inside[6],
        *inside[3:6],
        column_table,
        inside[0],
        unfinished,
    )

    gathered = lax.all_to_all(images, PLANE, 0, 0, tiled=True)
    places = jnp.stack([row_blocks[:, 0, 0], table_index[:, 0]])
    places = lax.all_gather(places, "layer").reshape(LAYERS * 2 * NDIR)
    mine = lax.axis_index("dir").astype(jnp.int32).reshape(1)
    feet = pl.pallas_call(
        feet_kernel,
        in_specs=[SCALARS, whole(CHUNKS * 2, STEPS, NM, 2, 8, LANES)],
        out_specs=whole(NM, NDIR * GROUP, PR),
        out_shape=jax.ShapeDtypeStruct((NM, NDIR * GROUP, PR), jnp.float32),
        compiler_params=room(24),
        cost_estimate=pl.CostEstimate(flops=0, bytes_accessed=100 * ROWS * COLS, transcendentals=0),
        name="feet",
    )(places, gathered.reshape(CHUNKS * 2, STEPS, NM, 2, 8, LANES))
    pupils = pl.pallas_call(
        pupil_kernel,
        in_specs=[SCALARS, whole(NM, NDIR * GROUP, PR), whole(NM, PR, PR)],
        out_specs=[whole(len(parts) * GROUP, PR) for parts in PARTS],
        out_shape=[jax.ShapeDtypeStruct((len(parts) * GROUP, PR), jnp.float32) for parts in PARTS],
        scratch_shapes=[pltpu.VMEM((NDIR, GROUP, PR), jnp.float32)],
        compiler_params=room(24),
        name="pupil",
    )(mine, feet, row_table)

    count = lax.axis_size("dir")
    send = lambda x, by: lax.ppermute(x, "dir", neighbours(count, by))
    far = send(pupils[4], -2)
    down3 = send(pupils[5], -2)
    up3 = send(pupils[3], 3)
    up2 = send(pupils[2], 2)
    up1 = send(pupils[1], 1)
    down2 = send(pupils[6] + far, -2)
    down1 = send(pupils[7] + down3, -1)
    terms = [pupils[0], up1, down1, up2, down2, up3]

    packed = pl.pallas_call(
        pack_kernel,
        in_specs=[whole(GROUP, PR)] * 6,
        out_specs=whole(CHUNKS, 8, LANES),
        out_shape=jax.ShapeDtypeStruct((CHUNKS, 8, LANES), jnp.float32),
        compiler_params=room(16),
        name="pack",
    )(*terms)
    rows = lax.all_to_all(packed, PLANE, 0, 0, tiled=True)
    slopes = pl.pallas_call(
        slope_kernel,
        in_specs=[whole(CHUNKS, 8, LANES)],
        out_specs=whole(STEPS, 2, 16, 1, PC),
        out_shape=jax.ShapeDtypeStruct((STEPS, 2, 16, 1, PC), jnp.float32),
        compiler_params=room(16),
        name="slopes",
    )(rows)
    return (screen_out[None], slopes)


def solution(mesh):
    return jax.shard_map(
        shards,
        mesh=mesh,
        in_specs=(
            P("layer", "strip", "dir"),
            P(None, "layer", "strip", "dir"),
            P("layer", None, "dir"),
            P("layer"),
            P(None, "layer", None),
            P(None, "layer"),
            P(),
            P(None, None, "dir"),
        ),
        out_specs=(P("layer", "strip", "dir"), P(None, None, ("layer", "strip"), "dir", None)),
        check_vma=False,
    )
```

```python
import jax
import jax.numpy as jnp
from jax import lax
from jax.experimental import pallas as pl
from jax.experimental.pallas import tpu as pltpu
from jax.sharding import PartitionSpec as P

ROWS = 256
COLS = 512
PR = 512
PC = 512
STEPS = 3
NM = 2
NDIR = 8
LAYERS = 4
STRIPS = 8
TAPS = 5
CHUNKS = LAYERS * STRIPS
PAD = 16
LANES = 128
GROUP = STEPS * 2 * 8
PLANE = ("layer", "strip")
PARTS = ((0,), (1,), (2,), (3,), (4,), (5,), (6,), (7,))


def advance(window, fresh, coef, shift):
    count = fresh.shape[0]
    moved = pltpu.roll(window, shift, axis=0)
    total = fresh.astype(jnp.float32)
    for k in range(TAPS):
        total = total + coef[k] * moved[8 + k : 8 + k + count, :]
    return total


def ends_kernel(screen, fresh, begin, last, screen_on, fresh_on):
    row = lax.broadcasted_iota(jnp.int32, (16, COLS), 0)
    first, final = fresh[1, 0:16, :], fresh[1, ROWS - 16 : ROWS, :]
    first = pltpu.roll(first.astype(jnp.float32), 12, axis=0)
    final = pltpu.roll(final.astype(jnp.float32), 4, axis=0)
    begin[0:16, :] = jnp.where(row < 12, screen[0:16, :], first)
    last[0:16, :] = jnp.where(row < 4, final, screen[ROWS - 16 : ROWS, :])
    begin[16:24, :] = fresh[0, 0:16, :].astype(jnp.float32)[0:8, :]
    last[16:24, :] = fresh[0, ROWS - 16 : ROWS, :].astype(jnp.float32)[8:16, :]
    screen_on[...] = screen[...]
    fresh_on[...] = fresh[...]


def inner_kernel(
    wind, screen, fresh, coef, flats, near0, fresh0, near1, near2, near3, coef_on, s3, s1, s2
):
    shift = wind[0] + 2
    coef_on[...] = coef[...]
    near0[0] = screen[0:16, :]
    near0[1] = screen[ROWS - 16 : ROWS, :]
    fresh0[0] = fresh[:, 0:32, :]
    fresh0[1] = fresh[:, ROWS - 32 : ROWS, :]
    steps = ((screen, s1, near1, 16, 16), (s1, s2, near2, 16, 16), (s2, s3, near3, 8, 32))
    for t, (src, dst, near, count, flat) in enumerate(steps):
        begin, end = 8 * (t + 1), ROWS - 8 * (t + 1)
        for r in range(begin, end, 64):
            stop = min(r + 64, end)
            for c in range(0, COLS, LANES):
                at = slice(c, c + LANES)
                low, high = r // 16 * 16, -(-stop // 16) * 16
                rows = fresh[t, low:high, at].astype(jnp.float32)[r - low : stop - low]
                dst[r:stop, at] = advance(
                    src[r - 8 : stop + 8, at], rows, coef[:, :, at], shift
                )
        near[0:count, :] = dst[begin : begin + count, :]
        near[count:, :] = dst[end - count : end, :]
        for r in range(flat, ROWS - flat, 32):
            stop = min(r + 32, ROWS - flat)
            flats[t, r:stop, :] = dst[r:stop, :].astype(jnp.bfloat16)


def outer_kernel(
    wind,
    near0,
    fresh0,
    low,
    high,
    coef,
    near1,
    near2,
    near3,
    table,
    inside,
    old,
    images,
    screen_out,
    flat,
    piece,
    ends,
    sem,
):
    shift = wind[0] + 2
    none = jnp.zeros((8, COLS), jnp.float32)
    join = lambda *rows: jnp.concatenate(rows, axis=0)
    after = lambda window, fresh: advance(window, fresh, coef, shift)
    leave = []

    def project(t):
        for m in range(NM):
            image = lax.dot_general(
                table[m], flat[t], (((1,), (1,)), ((), ())), preferred_element_type=jnp.float32
            )
            for half in range(2):
                for part in range(2):
                    at = image[half * 256 : half * 256 + 256, part * LANES : part * LANES + LANES]
                    piece[t, m, :, part, half, :, :] = at.reshape(CHUNKS, 8, LANES)
            copy = pltpu.make_async_copy(piece.at[t, m], images.at[:, :, t, m], sem.at[NM * t + m])
            copy.start()
            leave.append(copy)

    first, final = fresh0[0, 0].astype(jnp.float32), fresh0[1, 0].astype(jnp.float32)
    e = after(join(low[0:16, :], near0[0]), join(low[16:24, :], first[0:8]))
    f = after(join(near0[1], high[0:16, :]), join(final[24:32], high[16:24, :]))
    flat[0] = inside[0]
    flat[0, 0:16, :] = join(e[8:16], near1[0:8, :]).astype(jnp.bfloat16)
    flat[0, ROWS - 16 : ROWS, :] = join(near1[24:32, :], f[0:8]).astype(jnp.bfloat16)
    project(0)

    first, final = fresh0[0, 1].astype(jnp.float32), fresh0[1, 1].astype(jnp.float32)
    e = after(join(none, e, near1[0:16, :]), join(pltpu.roll(low[0:8, :], 4, axis=0), first[0:16]))
    f = after(join(near1[16:32, :], f, none), join(final[16:32], pltpu.roll(high[8:16, :], 4, axis=0)))
    flat[1] = inside[1]
    flat[1, 0:16, :] = e[8:24].astype(jnp.bfloat16)
    flat[1, ROWS - 16 : ROWS, :] = f[0:16].astype(jnp.bfloat16)
    project(1)

    first, final = fresh0[0, 2].astype(jnp.float32), fresh0[1, 2].astype(jnp.float32)
    e = after(join(e, near2[0:16, :]), first[0:24])
    f = after(join(near2[16:32, :], f), final[8:32])
    ends[0] = e
    ends[1] = f
    leave += [
        pltpu.make_async_copy(ends.at[0], screen_out.at[pl.ds(0, 24), :], sem.at[6]),
        pltpu.make_async_copy(ends.at[1], screen_out.at[pl.ds(ROWS - 24, 24), :], sem.at[7]),
    ]
    leave[-2].start()
    leave[-1].start()
    flat[2] = inside[2]
    flat[2, 0:32, :] = join(e, near3[0:8, :]).astype(jnp.bfloat16)
    flat[2, ROWS - 32 : ROWS, :] = join(near3[8:16, :], f).astype(jnp.bfloat16)
    project(2)
    for copy in leave:
        copy.wait()


def feet_kernel(places, x, feet):
    feet[...] = jnp.zeros(feet.shape, jnp.float32)
    lane = lax.broadcasted_iota(jnp.int32, (GROUP, LANES), 1)

    for layer in range(LAYERS):
        for d in range(NDIR):
            start = places[layer * 2 * NDIR + d]
            m = places[(layer * 2 + 1) * NDIR + d]
            block = start // 8
            shift = (start % 8) * 16
            back = (LANES - shift) % LANES
            rolled = []
            for i in range(5):
                rows = x[layer * 16 + (block + i) % 16, :, m]
                rolled.append(pltpu.roll(rows.reshape(GROUP, LANES), back, axis=1))
            for i in range(4):
                piece = jnp.where(lane < LANES - shift, rolled[i], rolled[i + 1])
                at = (m, pl.ds(d * GROUP, GROUP), pl.ds(i * LANES, LANES))
                feet[at] = feet[at] + piece


def pupil_kernel(mine, feet, table, *refs):
    *outs, pupils = refs
    total = None
    for m in range(NM):
        whole = feet[m]
        head = whole.astype(jnp.bfloat16)
        tail = (whole - head.astype(jnp.float32)).astype(jnp.bfloat16)
        for part in (head, tail):
            product = lax.dot_general(
                part, table[m], (((1,), (1,)), ((), ())), preferred_element_type=jnp.float32
            )
            total = product if total is None else total + product
    pupils[...] = total.reshape(pupils.shape)
    for out, parts in zip(outs, PARTS):
        for at, j in enumerate(parts):
            out[at * GROUP : at * GROUP + GROUP, :] = pupils[(mine[0] + j) % NDIR]


def pack_kernel(here, up1, down1, up2, down2, up3, out):
    total = here[...] + up1[...] + down1[...] + up2[...] + down2[...] + up3[...]
    tiles = [total[8 * j : 8 * j + 8] for j in range(6)]

    lane = lax.broadcasted_iota(jnp.int32, (8, LANES), 1)
    slot = lane // 16
    within = lane % 16
    heads = []
    for g in range(4):
        gathered = tiles[0][:, g * LANES : g * LANES + LANES]
        for j in range(1, 6):
            moved = pltpu.roll(tiles[j][:, g * LANES : g * LANES + LANES], j, axis=1)
            gathered = jnp.where(within == j, moved, gathered)
        heads.append(gathered)
    for g in range(4):
        for q in range(8):
            if q < 7:
                packed = pltpu.roll(heads[g], (96 - 16 * (q + 1)) % LANES, axis=1)
            elif g < 3:
                packed = pltpu.roll(heads[g + 1], 96, axis=1)
            else:
                packed = jnp.zeros((8, LANES), jnp.float32)
            for j in range(6):
                turn = (16 * j - 16 * q) % LANES
                moved = tiles[j][:, g * LANES : g * LANES + LANES]
                moved = moved if turn == 0 else pltpu.roll(moved, turn, axis=1)
                packed = jnp.where(slot == j, moved, packed)
            out[g * 8 + q] = packed


def slope_kernel(x, out):
    flipped = jnp.transpose(x[...].reshape(CHUNKS * 8, LANES))
    for t in range(STEPS):
        left = flipped[32 * t : 32 * t + 16]
        right = flipped[32 * t + 16 : 32 * t + 32]
        rows = jnp.concatenate([left, right], axis=1)
        edge = jnp.concatenate(
            [flipped[96 + 2 * t : 97 + 2 * t], flipped[97 + 2 * t : 98 + 2 * t]], axis=1
        )
        beside = jnp.concatenate([rows[:, 1:], jnp.zeros((16, 1), jnp.float32)], axis=1)
        below = jnp.concatenate([rows[1:], edge], axis=0)
        out[t, 0] = (beside - rows).reshape(16, 1, PC)
        out[t, 1] = (below - rows).reshape(16, 1, PC)


def neighbours(count, by):
    return [(i, (i + by) % count) for i in range(count)]


SCALARS = pl.BlockSpec(memory_space=pltpu.SMEM)


def room(mib):
    return pltpu.CompilerParams(vmem_limit_bytes=int(mib * 1024 * 1024))


def whole(*shape):
    return pl.BlockSpec(shape, lambda *_: (0,) * len(shape))


def shards(screen, innovation, coef, wind, row_blocks, table_index, row_table, column_table):
    state = screen[0]
    fresh = innovation[:, 0]
    strips = lax.axis_size("strip")

    halo = jax.ShapeDtypeStruct((24, COLS), jnp.float32)
    near = jax.ShapeDtypeStruct((32, COLS), jnp.float32)
    taps = jax.ShapeDtypeStruct((TAPS, 1, COLS), jnp.float32)
    begin, last, state, fresh = pl.pallas_call(
        ends_kernel,
        in_specs=[whole(ROWS, COLS), whole(STEPS, ROWS, COLS)],
        out_specs=[
            whole(24, COLS),
            whole(24, COLS),
            whole(ROWS, COLS),
            whole(STEPS, ROWS, COLS),
        ],
        out_shape=[
            halo,
            halo,
            jax.ShapeDtypeStruct((ROWS, COLS), jnp.float32),
            jax.ShapeDtypeStruct((STEPS, ROWS, COLS), jnp.bfloat16),
        ],
        compiler_params=room(24),
        name="ends",
    )(state, fresh)
    low = lax.ppermute(last, "strip", neighbours(strips, 1))
    high = lax.ppermute(begin, "strip", neighbours(strips, -1))

    *inside, unfinished = pl.pallas_call(
        inner_kernel,
        in_specs=[
            SCALARS,
            whole(ROWS, COLS),
            whole(STEPS, ROWS, COLS),
            whole(TAPS, 1, COLS),
        ],
        out_specs=[
            whole(STEPS, ROWS, COLS),
            whole(2, 16, COLS),
            whole(2, STEPS, 32, COLS),
            whole(32, COLS),
            whole(32, COLS),
            whole(16, COLS),
            whole(TAPS, 1, COLS),
            whole(ROWS, COLS),
        ],
        out_shape=[
            jax.ShapeDtypeStruct((STEPS, ROWS, COLS), jnp.bfloat16),
            jax.ShapeDtypeStruct((2, 16, COLS), jnp.float32),
            jax.ShapeDtypeStruct((2, STEPS, 32, COLS), jnp.bfloat16),
            near,
            near,
            jax.ShapeDtypeStruct((16, COLS), jnp.float32),
            taps,
            jax.ShapeDtypeStruct((ROWS, COLS), jnp.float32),
        ],
        scratch_shapes=[pltpu.VMEM((ROWS, COLS), jnp.float32)] * 2,
        compiler_params=room(24),
        cost_estimate=pl.CostEstimate(
            flops=12 * STEPS * ROWS * COLS, bytes_accessed=100 * ROWS * COLS, transcendentals=0
        ),
        name="inner",
    )(wind, state, fresh, jnp.swapaxes(coef, 0, 1))

    anywhere = pl.BlockSpec(memory_space=pl.ANY)
    images, screen_out = pl.pallas_call(
        outer_kernel,
        in_specs=[
            SCALARS,
            whole(2, 16, COLS),
            whole(2, STEPS, 32, COLS),
            whole(24, COLS),
            whole(24, COLS),
            whole(TAPS, 1, COLS),
            whole(32, COLS),
            whole(32, COLS),
            whole(16, COLS),
            whole(NM, PC, COLS),
            whole(STEPS, ROWS, COLS),
            anywhere,
        ],
        out_specs=[anywhere, anywhere],
        out_shape=[
            jax.ShapeDtypeStruct((CHUNKS, 2, STEPS, NM, 2, 8, LANES), jnp.float32),
            jax.ShapeDtypeStruct((ROWS, COLS), jnp.float32),
        ],
        input_output_aliases={11: 1},
        scratch_shapes=[
            pltpu.VMEM((STEPS, ROWS, COLS), jnp.bfloat16),
            pltpu.VMEM((STEPS, NM, CHUNKS, 2, 2, 8, LANES), jnp.float32),
            pltpu.VMEM((2, 24, COLS), jnp.float32),
            pltpu.SemaphoreType.DMA((8,)),
        ],
        compiler_params=room(50),
        name="outer",
    )(
        wind,
        *inside[1:3],
        low,
        high,
        inside[6],
        *inside[3:6],
        column_table,
        inside[0],
        unfinished,
    )

    gathered = lax.all_to_all(images, PLANE, 0, 0, tiled=True)
    places = jnp.stack([row_blocks[:, 0, 0], table_index[:, 0]])
    places = lax.all_gather(places, "layer").reshape(LAYERS * 2 * NDIR)
    mine = lax.axis_index("dir").astype(jnp.int32).reshape(1)
    feet = pl.pallas_call(
        feet_kernel,
        in_specs=[SCALARS, whole(CHUNKS * 2, STEPS, NM, 2, 8, LANES)],
        out_specs=whole(NM, NDIR * GROUP, PR),
        out_shape=jax.ShapeDtypeStruct((NM, NDIR * GROUP, PR), jnp.float32),
        compiler_params=room(24),
        cost_estimate=pl.CostEstimate(flops=0, bytes_accessed=100 * ROWS * COLS, transcendentals=0),
        name="feet",
    )(places, gathered.reshape(CHUNKS * 2, STEPS, NM, 2, 8, LANES))
    pupils = pl.pallas_call(
        pupil_kernel,
        in_specs=[SCALARS, whole(NM, NDIR * GROUP, PR), whole(NM, PR, PR)],
        out_specs=[whole(len(parts) * GROUP, PR) for parts in PARTS],
        out_shape=[jax.ShapeDtypeStruct((len(parts) * GROUP, PR), jnp.float32) for parts in PARTS],
        scratch_shapes=[pltpu.VMEM((NDIR, GROUP, PR), jnp.float32)],
        compiler_params=room(24),
        name="pupil",
    )(mine, feet, row_table)

    count = lax.axis_size("dir")
    send = lambda x, by: lax.ppermute(x, "dir", neighbours(count, by))
    far = send(pupils[4], -2)
    down3 = send(pupils[5], -2)
    up3 = send(pupils[3], 3)
    up2 = send(pupils[2], 2)
    up1 = send(pupils[1], 1)
    down2 = send(pupils[6] + far, -2)
    down1 = send(pupils[7] + down3, -1)
    terms = [pupils[0], up1, down1, up2, down2, up3]

    packed = pl.pallas_call(
        pack_kernel,
        in_specs=[whole(GROUP, PR)] * 6,
        out_specs=whole(CHUNKS, 8, LANES),
        out_shape=jax.ShapeDtypeStruct((CHUNKS, 8, LANES), jnp.float32),
        compiler_params=room(16),
        name="pack",
    )(*terms)
    rows = lax.all_to_all(packed, PLANE, 0, 0, tiled=True)
    slopes = pl.pallas_call(
        slope_kernel,
        in_specs=[whole(CHUNKS, 8, LANES)],
        out_specs=whole(STEPS, 2, 16, 1, PC),
        out_shape=jax.ShapeDtypeStruct((STEPS, 2, 16, 1, PC), jnp.float32),
        compiler_params=room(16),
        name="slopes",
    )(rows)
    return (screen_out[None], slopes)


def solution(mesh):
    return jax.shard_map(
        shards,
        mesh=mesh,
        in_specs=(
            P("layer", "strip", "dir"),
            P(None, "layer", "strip", "dir"),
            P("layer", None, "dir"),
            P("layer"),
            P(None, "layer", None),
            P(None, "layer"),
            P(),
            P(None, None, "dir"),
        ),
        out_specs=(P("layer", "strip", "dir"), P(None, None, ("layer", "strip"), "dir", None)),
        check_vma=False,
    )
```
